512 devices in a mesh: row: 64 (over z, y), col: 8 (over x, core).
Axes of the slice: x: 4, y: 8, z: 8, core: 2. Of those that a mesh axis runs over, the one named last changes fastest.
Arguments:
- giant_table: bfloat16 [65536, 128], P('row'), may hold values from -3 to 3
- look_row: int32 [131072], P(('row', 'col')), may hold values from 0 to 1023
- look_owner: int32 [131072, 1], P(('row', 'col')), may hold values from 0 to 63; in each aligned block of 256 rows (0 to 255, 256 to 511, ...) at most 8 rows name the same one
- look_bag: int32 [131072], P(('row', 'col')), may hold values from 0 to 31
- look_count: int32 [512], P(('row', 'col')), may hold values from 128 to 256, as said below
- medium_tables: bfloat16 [15, 256, 512], P(None, None, 'col'), may hold values from -3 to 3
- medium_ids: int32 [16384, 15, 4], P(('row', 'col')), may hold values from 0 to 255
- medium_lengths: int32 [16384, 15], P(('row', 'col')), may hold values from 1 to 4
- dense_features: bfloat16 [16384, 384], P(('row', 'col')), may hold values from -6 to 6
- click_labels: int32 [16384], P(('row', 'col')), may hold values 0 or 1
- cross_left: bfloat16 [8192, 512], P('col'), may hold values from -0.0625 to 0.0625
- cross_right: bfloat16 [512, 8192], P(None, 'col'), may hold values from -0.25 to 0.25
- cross_bias: float32 [8192], P('col'), may hold values from -3 to 3
- top_weight: float32 [8192], P('col'), may hold values from -0.0625 to 0.0625
Outputs:
- sample_grads: bfloat16 [16384, 512], P(('row', 'col'))
- giant_grad: float32 [65536, 128], P('row')
- medium_grad: float32 [15, 256, 512], P(None, None, 'col')
- left_grad: float32 [8192, 512], P(('col', 'row'))
- right_grad: float32 [512, 8192], P('row', 'col')
- bias_grad: float32 [8192], P('col')
- top_grad: float32 [8192], P('col')
The draws below stay inside these ranges and needn't reach their ends.
Inputs may be any that keep to these rules, and one draw needn't show every extreme that they name: `look_owner`: among the 256 slots of one device at most 8 name the same owner. `look_count`: some device has all 256 slots live.
All inputs are finite; a program needn't handle non-finite values. No bound on the sum of `click_labels` on one device may be relied on, other than what follows from the above.
Results may differ from the reference program's by a relative error of at most 0.015.
Values may be sent and summed in bfloat16 or wider, within the bound.
No kernel may reach another device: no remote copies, remote signals or barrier semaphores. Data moves between devices by JAX's collectives and lax.ppermute only.
A program may use at most 64 MiB of HBM per device.

```python
import math
import jax
import jax.numpy as jnp
import numpy as np
from jax import lax

HOST_B = 256
LOOK = 256
ROWS_DEV = 1024
MED_ROWS = 256
MED_T = 15
BAG = 4
EMB_DIM = 512
GIANT_DIM = 128
DENSE = 384
RANK = 512
B_DEV = 32
BATCH = 16384
CAP = 8
G_ROWS = 65536
PART = 512
CROSS = 8192
N_ROW = 64
N_COL = 8


def draw_look_count(key, part):
    key = jax.random.fold_in(key, 7)
    first, second = jax.random.split(key)
    counts = jax.random.randint(first, (N_ROW * N_COL,), LOOK // 2, LOOK + 1)
    chosen = jax.random.randint(second, (), 0, N_ROW * N_COL)
    return jnp.where(jnp.arange(N_ROW * N_COL) == chosen, LOOK, counts).astype(jnp.int32)


def with_ends(array, stream_key, smallest, top_value):
    spot = [jax.random.randint(jax.random.fold_in(stream_key, axis), (), 0, length) for axis, length in enumerate(array.shape)]
    main_axis = array.shape.index(max(array.shape))
    beside = spot[:main_axis] + [(spot[main_axis] + 1) % array.shape[main_axis]] + spot[main_axis + 1:]
    return array.at[tuple(spot)].set(smallest).at[tuple(beside)].set(top_value)


def level_of(rng, extent, pieces, low, largest):
    level = 1.0
    for axis_at, shards_of in pieces:
        heights = jax.random.uniform(jax.random.fold_in(jax.random.fold_in(rng, 6), axis_at), (shards_of,), jnp.float32, low / len(pieces), largest / len(pieces))
        level = level * jnp.repeat(jnp.exp(heights), extent[axis_at] // shards_of).reshape((-1,) + (1,) * (len(extent) - 1 - axis_at))
    return level


def cumulative_ranks(number_of, slope):
    loads = [(1 << 20) // math.isqrt(grade ** slope) + 1 for grade in range(1, number_of + 1)]
    width = 1 + sum(loads) // (1 << 30)
    return np.cumsum(np.array([max(1, weight // width) for weight in loads]))


def ranked(stream_key, dims, count, skew):
    table = cumulative_ranks(count, skew)
    ticket = jax.random.randint(jax.random.fold_in(stream_key, 1), dims, 0, int(table[count - 1]))
    rank = jnp.searchsorted(jnp.asarray(table, jnp.int32), ticket, side="right")
    return jax.random.permutation(jax.random.fold_in(stream_key, 2), count)[rank].astype(jnp.int32)


def assign_block(rng, own, number, rows, count, top, reach, skew):
    order = jax.random.permutation(rng, count)
    heavy_load, common = shares(count, rows * top, reach, skew, True), shares(count, rows * top, reach, skew, False)
    places = jnp.arange(count)

    def named(tallies, rotation):
        used = int((tallies > 0).sum())
        fixed = max(1, used // 4)
        shifted = fixed + (places - fixed + rotation * (used - fixed)) % max(1, count - fixed)
        return jnp.zeros((count,), jnp.int32).at[order[jnp.where(places < fixed, places, shifted)]].set(jnp.asarray(tallies, jnp.int32))

    tallies = jnp.where(number % 4 == 0, named(heavy_load, number // 4), named(common, number - number // 4 - 1))
    mixed = jax.random.permutation(jax.random.fold_in(own, 3), count)
    giver, receiver = mixed[0:count // 2 * 2:2], mixed[1:count // 2 * 2:2]
    room = jnp.minimum(tallies[giver] - 1, reach - tallies[receiver]) // 2
    room = jnp.where((giver == order[0]) | (receiver == order[0]) | (tallies[receiver] == 0), 0, jnp.maximum(room, 0))
    shifted = jax.random.randint(jax.random.fold_in(own, 4), (count // 2,), 0, 1 << 20) % (room + 1)
    tallies = tallies.at[giver].add(-shifted).at[receiver].add(shifted)
    members = jnp.searchsorted(jnp.cumsum(tallies), jnp.arange(rows * top), side="right").astype(jnp.int32)
    grid = members.reshape(top, rows).T
    grid = grid[jax.random.permutation(jax.random.fold_in(own, 1), rows)]
    rotation = jax.random.randint(jax.random.fold_in(own, 2), (rows, 1), 0, top)
    return jnp.take_along_axis(grid, (jnp.arange(top)[None, :] + rotation) % top, axis=1)


def shares(number_of, total, most, skew, full):
    weights = [(1 << 20) // math.isqrt(standing ** skew) + 1 for standing in range(1, number_of + 1)]
    largest = most if full else min(most, max(-(-total // number_of), total * weights[0] // sum(weights)))
    least = 1 if total - largest >= number_of - 1 else 0
    given, spare = [largest] + [least] * (number_of - 1), total - largest - least * (number_of - 1)
    while spare > 0:
        candidates = [i for i in range(1, number_of) if given[i] < largest] or [i for i in range(1, number_of) if given[i] < most]
        whole, remaining = sum([weights[i] for i in candidates]), spare
        for i in candidates:
            extra = min(most - given[i], max(1, remaining * weights[i] // whole), spare)
            given[i] = given[i] + extra
            spare = spare - extra
    return np.array(given)


def noise(key, extent, spread, bound, cuts=(), kind=jnp.bfloat16):
    entries = spread * jax.random.normal(key, extent, jnp.float32)
    if cuts:
        entries = entries * level_of(key, extent, cuts, -0.22, 0.18)
    return jnp.clip(entries, -bound, bound).astype(kind)


def setup_inputs(seed: int = 0) -> dict:
    key_list = jax.random.split(jax.random.key(seed), 15)
    giant_table = noise(key_list[0], (G_ROWS, GIANT_DIM), 0.5, 3.0, ((0, 64),))
    look_row = with_ends(ranked(key_list[1], (N_ROW * N_COL * LOOK,), ROWS_DEV, 2), jax.random.fold_in(key_list[1], 3), 0, ROWS_DEV - 1).astype(jnp.int32)
    look_owner_keys = jax.random.split(jax.random.fold_in(key_list[2], 1), (N_ROW * N_COL * LOOK) // LOOK)
    look_owner_turns = jax.random.permutation(jax.random.fold_in(key_list[2], 3), (N_ROW * N_COL * LOOK) // LOOK)
    look_owner = jax.vmap(lambda own, number: assign_block(jax.random.fold_in(key_list[2], 2), own, number, LOOK, N_ROW, 1, CAP, 2))(look_owner_keys, look_owner_turns).reshape((N_ROW * N_COL * LOOK, 1))
    look_bag = with_ends(jax.random.randint(key_list[3], (N_ROW * N_COL * LOOK,), 0, B_DEV), jax.random.fold_in(key_list[3], 1), 0, B_DEV - 1).astype(jnp.int32)
    look_count = draw_look_count(jax.random.fold_in(key_list[14], 71), 0)
    medium_tables = noise(key_list[5], (MED_T, MED_ROWS, EMB_DIM), 0.5, 3.0, ((2, 8),))
    medium_ids = with_ends(ranked(key_list[6], (BATCH, MED_T, BAG), MED_ROWS, 2), jax.random.fold_in(key_list[6], 3), 0, MED_ROWS - 1).astype(jnp.int32)
    medium_lengths = with_ends(jax.random.randint(key_list[7], (BATCH, MED_T), 1, BAG + 1), jax.random.fold_in(key_list[7], 1), 1, BAG).astype(jnp.int32)
    dense_features = noise(key_list[8], (BATCH, DENSE), 1.0, 6.0, ((0, 512),))
    click_labels = with_ends((jax.random.randint(key_list[9], (BATCH,), 0, 4) < 1).astype(jnp.int32), jax.random.fold_in(key_list[9], 1), 0, 1)
    cross_left = noise(key_list[10], (CROSS, RANK), CROSS ** -0.5, 0.0625, ((0, 8),))
    cross_right = noise(key_list[11], (RANK, CROSS), RANK ** -0.5, 0.25, ((1, 8),))
    cross_bias = noise(key_list[12], (CROSS,), 0.5, 3.0, ((0, 8),), jnp.float32)
    top_weight = noise(key_list[13], (CROSS,), CROSS ** -0.5, 0.0625, ((0, 8),), jnp.float32)
    return {"giant_table": giant_table, "look_row": look_row, "look_owner": look_owner, "look_bag": look_bag, "look_count": look_count, "medium_tables": medium_tables, "medium_ids": medium_ids, "medium_lengths": medium_lengths, "dense_features": dense_features, "click_labels": click_labels, "cross_left": cross_left, "cross_right": cross_right, "cross_bias": cross_bias, "top_weight": top_weight}


LOSS_SCALE = 0.015625


def giant_slots(look_row, look_owner, look_bag, look_count):
    slot_index = jnp.arange(N_ROW * N_COL * LOOK, dtype=jnp.int32)
    device = slot_index // LOOK
    slot_valid = ((slot_index % LOOK) < look_count[device]).astype(jnp.float32)
    table_row = (device // N_COL) * ROWS_DEV + look_row
    sample = (look_owner[:, 0] * N_COL + device % N_COL) * B_DEV + look_bag
    return slot_valid, table_row.astype(jnp.int32), sample.astype(jnp.int32)


def reference(giant_table, look_row, look_owner, look_bag, look_count, medium_tables, medium_ids, medium_lengths, dense_features, click_labels, cross_left, cross_right, cross_bias, top_weight):
    slot_valid, table_row, sample = giant_slots(look_row, look_owner, look_bag, look_count)
    looked = giant_table[table_row].astype(jnp.float32) * slot_valid[:, None]
    pooled = jax.ops.segment_sum(looked, sample, num_segments=BATCH).astype(jnp.bfloat16)
    sample_part = jnp.concatenate([pooled, dense_features], axis=1)
    slice_width = EMB_DIM // N_COL
    part_width = PART // N_COL
    medium_width = MED_T * slice_width
    block_width = medium_width + part_width

    def host_step(totals, inputs):
        grad_left, grad_right, grad_bias, grad_top, grad_medium = totals
        host_part, host_ids, host_lengths, host_labels = inputs
        looked_medium = jnp.stack([medium_tables[table_index][host_ids[:, table_index, :]] for table_index in range(MED_T)], axis=1)
        bag_mask = (jnp.arange(BAG, dtype=jnp.int32)[None, None, :] < host_lengths[:, :, None]).astype(jnp.float32)
        embedded = jnp.sum(looked_medium.astype(jnp.float32) * bag_mask[..., None], axis=2).astype(jnp.bfloat16)
        blocks = []
        for column in range(N_COL):
            blocks.append(embedded[:, :, column * slice_width:(column + 1) * slice_width].reshape(HOST_B, medium_width))
            blocks.append(host_part[:, column * part_width:(column + 1) * part_width])
        crossed_in = jnp.concatenate(blocks, axis=1)
        inputs_wide = crossed_in.astype(jnp.float32)
        low_rank = jnp.dot(crossed_in, cross_left, preferred_element_type=jnp.float32).astype(jnp.bfloat16)
        expanded = jnp.dot(low_rank, cross_right, preferred_element_type=jnp.float32) + cross_bias
        crossed = inputs_wide * expanded + inputs_wide
        logits = jnp.sum(crossed * top_weight, axis=1)
        residue = (jax.nn.sigmoid(logits) - host_labels.astype(jnp.float32)) * LOSS_SCALE
        grad_crossed = residue[:, None] * top_weight
        grad_expanded = grad_crossed * inputs_wide
        grad_expanded_low = grad_expanded.astype(jnp.bfloat16)
        grad_top = grad_top + jnp.sum(residue[:, None] * crossed, axis=0)
        grad_bias = grad_bias + jnp.sum(grad_expanded, axis=0)
        grad_right = grad_right + jnp.dot(low_rank.T, grad_expanded_low, preferred_element_type=jnp.float32)
        grad_rank = jnp.dot(grad_expanded_low, cross_right.T, preferred_element_type=jnp.float32).astype(jnp.bfloat16)
        grad_left = grad_left + jnp.dot(crossed_in.T, grad_rank, preferred_element_type=jnp.float32)
        grad_inputs = (grad_crossed * (expanded + 1.0) + jnp.dot(grad_rank, cross_left.T, preferred_element_type=jnp.float32)).astype(jnp.bfloat16)
        medium_pieces = []
        part_pieces = []
        for column in range(N_COL):
            offset = column * block_width
            medium_pieces.append(grad_inputs[:, offset:offset + medium_width].reshape(HOST_B, MED_T, slice_width))
            part_pieces.append(grad_inputs[:, offset + medium_width:offset + block_width])
        grad_embedded = jnp.concatenate(medium_pieces, axis=2).astype(jnp.float32)
        table_ids = jnp.broadcast_to(jnp.arange(MED_T, dtype=jnp.int32)[None, :, None], host_ids.shape)
        grad_medium = grad_medium.at[table_ids, host_ids].add(grad_embedded[:, :, None, :] * bag_mask[..., None])
        return (grad_left, grad_right, grad_bias, grad_top, grad_medium), jnp.concatenate(part_pieces, axis=1)

    start_totals = (jnp.zeros((CROSS, RANK), jnp.float32), jnp.zeros((RANK, CROSS), jnp.float32), jnp.zeros((CROSS,), jnp.float32), jnp.zeros((CROSS,), jnp.float32), jnp.zeros((MED_T, MED_ROWS, EMB_DIM), jnp.float32))
    host_inputs = (sample_part.reshape(N_ROW, HOST_B, PART), medium_ids.reshape(N_ROW, HOST_B, MED_T, BAG), medium_lengths.reshape(N_ROW, HOST_B, MED_T), click_labels.reshape(N_ROW, HOST_B))
    totals, part_grads = lax.scan(host_step, start_totals, host_inputs)
    left_grad, right_grad, bias_grad, top_grad, medium_grad = totals
    sample_grads = part_grads.reshape(BATCH, PART)
    slot_grads = sample_grads[sample, :GIANT_DIM].astype(jnp.float32) * slot_valid[:, None]
    giant_grad = jax.ops.segment_sum(slot_grads, table_row, num_segments=G_ROWS)
    return (sample_grads, giant_grad, medium_grad, left_grad, right_grad, bias_grad, top_grad)
```

```python
import functools

import jax
import jax.numpy as jnp
from jax import lax
from jax.experimental import pallas as pl
from jax.experimental.pallas import tpu as pltpu
from jax.sharding import PartitionSpec as P

LOSS_SCALE = 0.015625
F32, BF16, I32 = jnp.float32, jnp.bfloat16, jnp.int32
ROWS, COLS = 64, 8
SIDE = 8
BATCH, HOST = 32, 256
SLOTS, CAP = 256, 8
WIDE, RANK = 1024, 512
TABLES, NAMES, SLICE = 15, 256, 64
BLOCK = 128

NN = ((1,), (0,))
NT = ((1,), (1,))
TN = ((0,), (0,))


def dot(left, right, dims):
    return lax.dot_general(left, right, (dims, ((), ())), preferred_element_type=F32)


def lanes(shape):
    return lax.broadcasted_iota(I32, shape, len(shape) - 1)


def subs(shape):
    return lax.broadcasted_iota(I32, shape, len(shape) - 2)


def one_hot(mask):
    return jnp.where(mask, 1.0, 0.0).astype(BF16)


def call(kernel, outs, *args, smem=(), scratch=()):
    return pl.pallas_call(
        kernel,
        out_shape=outs,
        in_specs=[
            pl.BlockSpec(memory_space=pltpu.SMEM if i in smem else pltpu.VMEM)
            for i in range(len(args))
        ],
        out_specs=jax.tree.map(lambda _: pl.BlockSpec(memory_space=pltpu.VMEM), outs),
        scratch_shapes=list(scratch),
        compiler_params=pltpu.CompilerParams(vmem_limit_bytes=48 * 2**20),
    )(*args)


def struct(shape, dtype):
    return jax.ShapeDtypeStruct(shape, dtype)


def route_kernel(count_ref, row_ref, owner_ref, bag_ref, table_ref, send_ref, names_ref):
    eye = subs((SLOTS, SLOTS)) == lanes((SLOTS, SLOTS))

    def column(ref):
        return jnp.sum(jnp.where(eye, ref[...].astype(F32), 0.0), axis=1, keepdims=True)

    row, bag = column(row_ref), column(bag_ref)
    owner = owner_ref[...]
    live = subs((SLOTS, BLOCK)) < count_ref[0]
    hits = jnp.where((owner == lanes((SLOTS, BLOCK))) & live, 1.0, 0.0)
    before = one_hot(subs((SLOTS, SLOTS)) > lanes((SLOTS, SLOTS)))
    earlier = dot(before, hits.astype(BF16), NN)
    place = jnp.sum(earlier * hits, axis=1, keepdims=True)
    alive = jnp.sum(hits, axis=1, keepdims=True)
    target = jnp.where(alive > 0.5, owner.astype(F32) * CAP + place, -1.0)
    at = target == lanes((SLOTS, ROWS * CAP)).astype(F32)
    looked = dot(one_hot(row == lanes((SLOTS, 1024)).astype(F32)), table_ref[...], NN)
    both = jnp.concatenate(
        [looked.astype(BF16), jnp.broadcast_to(bag, (SLOTS, BLOCK)).astype(BF16)], axis=1
    )
    sent = dot(one_hot(at), both, TN)
    send_ref[...] = jnp.concatenate(
        [
            sent[:, :BLOCK].reshape(ROWS, CAP, BLOCK),
            sent[:, BLOCK:].reshape(ROWS, CAP, BLOCK),
        ],
        axis=1,
    ).astype(BF16)
    named = jnp.sum(jnp.where(at, row + 1.0, 0.0), axis=0, keepdims=True)
    high = jnp.floor(named * (1.0 / 32.0))
    low = named - 32.0 * high
    names_ref[...] = jnp.concatenate(
        [part[:, i * BLOCK : (i + 1) * BLOCK] for part in (high, low) for i in range(4)], axis=0
    )


def pool_kernel(got_ref, dense_ref, ids_ref, names_ref, out_ref):
    got = got_ref[...].astype(F32)
    data = got[:, :CAP].reshape(ROWS * CAP, BLOCK).astype(BF16)
    bags = got[:, CAP:].reshape(ROWS * CAP, BLOCK)
    hot = one_hot(bags == lanes((ROWS * CAP, BLOCK)).astype(F32))
    pooled = dot(hot, data, TN)[:BATCH].astype(BF16).astype(F32)
    eye = subs((BLOCK, BLOCK)) == lanes((BLOCK, BLOCK))
    bag_rows = [
        jnp.sum(jnp.where(eye, bags[i * BLOCK : (i + 1) * BLOCK], 0.0), axis=0, keepdims=True)
        for i in range(4)
    ]
    meta = jnp.concatenate(bag_rows + [names_ref[...], jnp.zeros((4, BLOCK), F32)], axis=0)
    part = jnp.concatenate([pooled, dense_ref[...].astype(F32)], axis=1)
    ids = ids_ref[...].astype(F32)
    for c in range(COLS):
        top = jnp.concatenate([part[:, c * SLICE : (c + 1) * SLICE], ids], axis=1)
        out_ref[c] = jnp.concatenate([top, meta], axis=0).astype(BF16)


def cross_kernel(
    got_ref, tables_ref, left_ref, right_ref, weight_ref, bias_ref, out_ref, x_ref, counts_ref
):
    ids = got_ref[:, :BATCH, SLICE:].astype(F32).reshape(HOST, SLICE)
    part = got_ref[:, :BATCH, :SLICE].astype(F32).reshape(HOST, SLICE)
    name = lanes((HOST, NAMES)).astype(F32)
    pieces = []
    for t in range(TABLES):
        count = jnp.zeros((HOST, NAMES), F32)
        for j in range(4):
            count += jnp.where(ids[:, 4 * t + j : 4 * t + j + 1] == name, 1.0, 0.0)
        low = count.astype(BF16)
        counts_ref[t] = low
        pieces.append(dot(low, tables_ref[t], NN))
        if t % 2:
            x_ref[:, (t // 2) * BLOCK : (t // 2 + 1) * BLOCK] = jnp.concatenate(
                pieces, axis=1
            ).astype(BF16)
            pieces = []
    x_ref[:, WIDE - BLOCK :] = jnp.concatenate(pieces + [part], axis=1).astype(BF16)
    low_rank = jnp.zeros((HOST, RANK), F32)
    back = jnp.zeros((HOST, RANK), F32)
    plain = jnp.zeros((HOST, 1), F32)
    for n in range(4):
        cols = slice(n * 256, (n + 1) * 256)
        x = x_ref[:, cols]
        weighted = x.astype(F32) * weight_ref[:, cols]
        low_rank += dot(x, left_ref[cols, :], NN)
        back += dot(weighted.astype(BF16), right_ref[:, cols], NT)
        plain += jnp.sum(weighted * (bias_ref[:, cols] + 1.0), axis=1, keepdims=True)
    high = plain.astype(BF16).astype(F32)
    lane = lanes((HOST, BLOCK))
    rest = jnp.where(lane == 0, high, jnp.where(lane == 1, plain - high, 0.0))
    out_ref[:, :, :RANK] = low_rank.astype(BF16).reshape(COLS, BATCH, RANK)
    out_ref[:, :, RANK : 2 * RANK] = back.astype(BF16).reshape(COLS, BATCH, RANK)
    out_ref[:, :, 2 * RANK :] = rest.astype(BF16).reshape(COLS, BATCH, BLOCK)


def residue_kernel(got_ref, label_ref, out_ref):
    total = got_ref[0].astype(F32)
    for c in range(1, COLS):
        total += got_ref[c].astype(F32)
    low_rank = total[:, :RANK].astype(BF16).astype(F32)
    back = total[:, RANK : 2 * RANK]
    plain = total[:, 2 * RANK : 2 * RANK + 1] + total[:, 2 * RANK + 1 : 2 * RANK + 2]
    logits = jnp.sum(low_rank * back, axis=1, keepdims=True) + plain
    residue = (jax.nn.sigmoid(logits) - label_ref[...].astype(F32)) * LOSS_SCALE
    high = residue.astype(BF16).astype(F32)
    lane = lanes((BATCH, BLOCK))
    rest = jnp.where(lane == 0, high, jnp.where(lane == 1, residue - high, 0.0))
    block = jnp.concatenate([low_rank, residue * back, rest], axis=1).astype(BF16)
    for c in range(COLS):
        out_ref[c] = block


def part_kernel(got_ref, x_ref, left_ref, right_ref, weight_ref, bias_ref, out_ref):
    last = slice(WIDE - BLOCK, WIDE)
    low_rank = got_ref[:, :, :RANK].reshape(HOST, RANK)
    grad_rank = got_ref[:, :, RANK : 2 * RANK].reshape(HOST, RANK)
    rest = got_ref[:, :, 2 * RANK :].astype(F32).reshape(HOST, BLOCK)
    residue = rest[:, 0:1] + rest[:, 1:2]
    expanded = dot(low_rank, right_ref[:, last], NN) + bias_ref[:, last]
    grad = residue * weight_ref[:, last] * (expanded + 1.0) + dot(grad_rank, left_ref[last, :], NT)
    grad = grad[:, SLICE:].astype(BF16).astype(F32)
    blank = jnp.zeros((BATCH, SLICE), F32)
    for c in range(COLS):
        k = (c % 4) * 16
        own = jnp.concatenate([grad[c * BATCH : (c + 1) * BATCH], blank], axis=1)
        bag = jnp.concatenate(
            [grad[i * BATCH : (i + 1) * BATCH, k : k + 16] for i in range(COLS)], axis=1
        )
        out_ref[c] = jnp.concatenate([own, bag], axis=0).astype(BF16)


def grads_kernel(
    place_ref,
    got_ref,
    part_ref,
    meta_ref,
    x_ref,
    counts_ref,
    left_ref,
    right_ref,
    weight_ref,
    bias_ref,
    out_ref,
    sample_ref,
    right_scr,
):
    odd = place_ref[0]
    low_rank = got_ref[:, :, :RANK].reshape(HOST, RANK)
    grad_rank = got_ref[:, :, RANK : 2 * RANK].reshape(HOST, RANK)
    rest = got_ref[:, :, 2 * RANK :].astype(F32).reshape(HOST, BLOCK)
    residue = rest[:, 0:1] + rest[:, 1:2]

    def at(r):
        z, y = r // SIDE, r % SIDE
        return jnp.where(odd == 1, z, y), jnp.where(odd == 1, y, z)

    biases, tops = [], []
    for n in range(4):
        cols = slice(n * 256, (n + 1) * 256)
        x = x_ref[:, cols]
        wide = x.astype(F32)
        expanded = dot(low_rank, right_ref[:, cols], NN) + bias_ref[:, cols]
        tops.append(jnp.sum(residue * (wide * expanded + wide), axis=0, keepdims=True))
        grad_crossed = residue * weight_ref[:, cols]
        grad_expanded = grad_crossed * wide
        biases.append(jnp.sum(grad_expanded, axis=0, keepdims=True))
        right_scr[:, cols] = dot(low_rank, grad_expanded.astype(BF16), TN)
        left = dot(x, grad_rank, TN).astype(BF16)
        grad = grad_crossed * (expanded + 1.0) + dot(grad_rank, left_ref[cols, :], NT)
        grad = grad.astype(BF16)
        for i in range(16):
            a, b = at(16 * n + i)
            out_ref[a, b, :, :RANK] = left[16 * i : 16 * i + 16]
        for i in range(4):
            t = 4 * n + i
            if t < TABLES:
                medium = dot(grad[:, i * SLICE : (i + 1) * SLICE], counts_ref[t], TN).astype(BF16)
            else:
                medium = jnp.zeros((SLICE, NAMES), BF16)
            for k in range(4):
                a, b = at(4 * t + k)
                out_ref[a, b, :, 2 * RANK : 2 * RANK + NAMES] = medium[16 * k : 16 * k + 16]
    for r in range(ROWS):
        a, b = at(r)
        band = right_scr[8 * r : 8 * r + 8, :]
        out_ref[a, b, :, RANK : 2 * RANK] = jnp.concatenate(
            [band[:, :RANK], band[:, RANK:]], axis=0
        ).astype(BF16)

    bags = [
        jnp.concatenate(
            [meta_ref[c, BATCH : BATCH + 16, :].astype(F32)[i : i + 1] for i in range(4)], axis=1
        )
        for c in range(COLS)
    ]
    bag = subs((BATCH, ROWS * CAP)).astype(F32)
    hot = jnp.concatenate([jnp.where(b == bag, 1.0, 0.0) for b in bags], axis=0).astype(BF16)
    own = jnp.where(
        place_ref[1] == 1,
        part_ref[1, BATCH:, :].astype(F32),
        part_ref[0, BATCH:, :].astype(F32),
    )
    spread = jnp.concatenate([own] * COLS, axis=0)
    spread = jnp.where(
        subs((HOST, BLOCK)) // BATCH == lanes((HOST, BLOCK)) // 16, spread, 0.0
    ).astype(BF16)
    back = dot(hot, spread, TN).reshape(ROWS, CAP, BLOCK)
    back = jnp.concatenate([back[:, :, :SLICE], back[:, :, SLICE:]], axis=1)

    bias = jnp.concatenate(biases, axis=1)
    top = jnp.concatenate(tops, axis=1)
    blank = jnp.zeros((12, SLICE), F32)
    vectors = []
    for b in range(SIDE):
        pieces = [
            v[:, b * BLOCK + h * SLICE : b * BLOCK + (h + 1) * SLICE]
            for v in (bias, top)
            for h in range(2)
        ]
        vectors.append(jnp.concatenate(pieces + [blank], axis=0))
    vectors = jnp.stack(vectors, axis=0)
    out_ref[:, :, :, 2 * RANK + NAMES : 2 * RANK + NAMES + SLICE] = jnp.broadcast_to(
        vectors[None], (SIDE, SIDE, 16, SLICE)
    ).astype(BF16)
    low = back.astype(BF16)
    for r in range(ROWS):
        a, b = at(r)
        out_ref[a, b, :, 2 * RANK + NAMES + SLICE :] = low[r]
    sample_ref[...] = jnp.concatenate(
        [part_ref[c, :BATCH, :SLICE].astype(F32) for c in range(COLS)], axis=1
    ).astype(BF16)


SUMS = 2 * RANK + NAMES


def middle_kernel(got_ref, out_ref):
    vectors = []
    for b in range(SIDE):
        total = got_ref[0, b].astype(F32)
        for a in range(1, SIDE):
            total += got_ref[a, b].astype(F32)
        out_ref[b, :, :SUMS] = total[:, :SUMS].astype(BF16)
        vectors.append(total[:4, SUMS : SUMS + SLICE])
        for a in range(0, SIDE, 2):
            pair = [got_ref[a + i, b, :, SUMS + SLICE :].astype(F32) for i in range(2)]
            at = SUMS + a * SLICE
            out_ref[b, :, at : at + BLOCK] = jnp.concatenate(pair, axis=1).astype(BF16)
    packed = jnp.concatenate(
        [jnp.concatenate(vectors[:4], axis=0), jnp.concatenate(vectors[4:], axis=0)], axis=1
    ).astype(BF16)
    for b in range(SIDE):
        out_ref[b, :, SUMS + 512 :] = packed


def last_kernel(
    place_ref,
    got_ref,
    meta_ref,
    left_ref,
    right_ref,
    bias_ref,
    top_ref,
    giant_ref,
    medium_ref,
    data_scr,
):
    odd = place_ref[0]
    sums = got_ref[0, :, :SUMS].astype(F32)
    packed = got_ref[0, :, SUMS + 512 :].astype(F32)
    for a in range(1, SIDE):
        sums += got_ref[a, :, :SUMS].astype(F32)
        packed += got_ref[a, :, SUMS + 512 :].astype(F32)
    left_ref[...] = sums[:, :RANK]
    right = sums[:, RANK : 2 * RANK]
    right_ref[...] = jnp.concatenate([right[:8], right[8:]], axis=1)
    medium = sums[:, 2 * RANK :].astype(BF16)
    for r in range(ROWS):
        medium_ref[r] = medium
    for v, ref in ((0, bias_ref), (2, top_ref)):
        pieces = []
        for b in range(SIDE):
            at = (b // 4) * SLICE
            for h in range(2):
                i = 4 * (b % 4) + v + h
                pieces.append(packed[i : i + 1, at : at + SLICE])
        ref[...] = jnp.concatenate(pieces, axis=1)

    for second in range(SIDE):
        for first in range(SIDE):
            at = SUMS + first * SLICE
            block = got_ref[second, :, at : at + SLICE].astype(F32)
            r = jnp.where(odd == 1, first * SIDE + second, second * SIDE + first)
            data_scr[r] = jnp.concatenate([block[:CAP], block[CAP:]], axis=1)
    data = data_scr[...].reshape(ROWS * CAP, BLOCK)
    group = lanes((ROWS * CAP, BLOCK)) // 16
    row = subs((1024, ROWS * CAP)).astype(F32) + 1.0
    total = jnp.zeros((1024, BLOCK), F32)
    for c in range(COLS):
        meta = meta_ref[c, BATCH : BATCH + 16, :].astype(F32)
        name = jnp.concatenate(
            [meta[4 + i : 5 + i] * 32.0 + meta[8 + i : 9 + i] for i in range(4)], axis=1
        )
        total += dot(one_hot(name == row), jnp.where(group == c, data, 0.0).astype(BF16), NN)
    for shift in (64, 32, 16):
        total = total + pltpu.roll(total, shift, 1)
    slot = lanes((BLOCK, BLOCK)) // 16
    packed = jnp.zeros((BLOCK, BLOCK), F32)
    for i in range(8):
        packed = jnp.where(slot == i, total[i * BLOCK : (i + 1) * BLOCK], packed)
    packed = packed.astype(BF16)
    for c in range(COLS):
        giant_ref[c] = packed


def giant_kernel(got_ref, out_ref):
    slot = lanes((BLOCK, BLOCK)) // 16
    for i in range(8):
        block = jnp.zeros((BLOCK, BLOCK), F32)
        for c in range(COLS):
            piece = got_ref[c].astype(F32)
            shift = ((c - i) * 16) % BLOCK
            if shift:
                piece = pltpu.roll(piece, shift, 1)
            block = jnp.where(slot == c, piece, block)
        out_ref[i * BLOCK : (i + 1) * BLOCK, :] = block


def medium_kernel(got_ref, out_ref):
    for t in range(TABLES):
        block = got_ref[4 * t : 4 * t + 4].astype(F32).reshape(SLICE, NAMES)
        out_ref[t] = block.T


def sides():
    first, second = [], []
    for c in range(COLS):
        for k in range(SIDE):
            along_y = [(k * SIDE + y) * COLS + c for y in range(SIDE)]
            along_z = [(z * SIDE + k) * COLS + c for z in range(SIDE)]
            first.append(along_z if c % 2 else along_y)
            second.append(along_y if c % 2 else along_z)
    return first, second


def swap(value, axis, groups=None):
    return lax.all_to_all(
        value, axis, split_axis=0, concat_axis=0, tiled=True, axis_index_groups=groups
    )


def body(
    giant_table,
    look_row,
    look_owner,
    look_bag,
    look_count,
    medium_tables,
    medium_ids,
    medium_lengths,
    dense_features,
    click_labels,
    cross_left,
    cross_right,
    cross_bias,
    top_weight,
):
    first, second = sides()
    col = lax.axis_index("col")
    place = jnp.stack([col % 2, col // 4]).astype(I32)
    bias, weight = cross_bias.reshape(1, WIDE), top_weight.reshape(1, WIDE)
    live = jnp.arange(4)[None, None, :] < medium_lengths[:, :, None]
    ids = jnp.where(live, medium_ids, NAMES).reshape(BATCH, 4 * TABLES).astype(BF16)
    ids = jnp.pad(ids, ((0, 0), (0, SLICE - 4 * TABLES)))

    send, names = call(
        route_kernel,
        (struct((ROWS, 2 * CAP, BLOCK), BF16), struct((8, BLOCK), F32)),
        look_count,
        look_row.reshape(1, SLOTS),
        look_owner,
        look_bag.reshape(1, SLOTS),
        giant_table,
        smem=(0,),
    )
    got = swap(send, "row")
    send = call(
        pool_kernel, struct((COLS, 48, BLOCK), BF16), got, dense_features, ids, names
    )
    meta = swap(send, "col")
    send, x, counts = call(
        cross_kernel,
        (
            struct((COLS, BATCH, 2 * RANK + BLOCK), BF16),
            struct((HOST, WIDE), BF16),
            struct((TABLES, HOST, NAMES), BF16),
        ),
        meta,
        medium_tables,
        cross_left,
        cross_right,
        weight,
        bias,
    )
    got = swap(send, "col")
    send = call(
        residue_kernel,
        struct((COLS, BATCH, 2 * RANK + BLOCK), BF16),
        got,
        click_labels.reshape(BATCH, 1),
    )
    ranks = swap(send, "col")
    send = call(
        part_kernel,
        struct((COLS, 2 * BATCH, BLOCK), BF16),
        ranks,
        x,
        cross_left,
        cross_right,
        weight,
        bias,
    )
    parts = swap(send, "col")
    send, sample_grads = call(
        grads_kernel,
        (
            struct((SIDE, SIDE, 16, SUMS + BLOCK), BF16),
            struct((BATCH, COLS * SLICE), BF16),
        ),
        place,
        ranks,
        parts,
        meta,
        x,
        counts,
        cross_left,
        cross_right,
        weight,
        bias,
        smem=(0,),
        scratch=(pltpu.VMEM((RANK, WIDE), F32),),
    )
    got = swap(send, ("row", "col"), first)
    send = call(middle_kernel, struct((SIDE, 16, SUMS + 512 + BLOCK), BF16), got)
    got = swap(send, ("row", "col"), second)
    left_grad, right_grad, bias_grad, top_grad, giant, medium = call(
        last_kernel,
        (
            struct((16, RANK), F32),
            struct((8, WIDE), F32),
            struct((1, WIDE), F32),
            struct((1, WIDE), F32),
            struct((COLS, BLOCK, BLOCK), BF16),
            struct((ROWS, 16, NAMES), BF16),
        ),
        place,
        got,
        meta,
        smem=(0,),
        scratch=(pltpu.VMEM((ROWS, CAP, BLOCK), F32),),
    )
    giant_grad = call(giant_kernel, struct((1024, BLOCK), F32), swap(giant, "col"))
    medium_grad = call(
        medium_kernel, struct((TABLES, NAMES, SLICE), F32), swap(medium, "row")
    )
    return (
        sample_grads,
        giant_grad,
        medium_grad,
        left_grad,
        right_grad,
        bias_grad.reshape(WIDE),
        top_grad.reshape(WIDE),
    )


def solution(mesh):
    both = P(("row", "col"))
    placed = (
        P("row", None),
        both,
        P(("row", "col"), None),
        both,
        both,
        P(None, None, "col"),
        P(("row", "col"), None, None),
        P(("row", "col"), None),
        P(("row", "col"), None),
        both,
        P("col", None),
        P(None, "col"),
        P("col"),
        P("col"),
    )
    return jax.shard_map(
        body,
        mesh=mesh,
        in_specs=placed,
        out_specs=(
            P(("row", "col"), None),
            P("row", None),
            P(None, None, "col"),
            P(("col", "row"), None),
            P("row", "col"),
            P("col"),
            P("col"),
        ),
        check_vma=False,
    )
```

```python
import functools

import jax
import jax.numpy as jnp
from jax import lax
from jax.experimental import pallas as pl
from jax.experimental.pallas import tpu as pltpu
from jax.sharding import PartitionSpec as P

LOSS_SCALE = 0.015625
F32, BF16, I32 = jnp.float32, jnp.bfloat16, jnp.int32
ROWS, COLS = 64, 8
SIDE = 8
BATCH, HOST = 32, 256
SLOTS, CAP = 256, 8
WIDE, RANK = 1024, 512
TABLES, NAMES, SLICE = 15, 256, 64
BLOCK = 128

NN = ((1,), (0,))
NT = ((1,), (1,))
TN = ((0,), (0,))


def dot(left, right, dims):
    return lax.dot_general(left, right, (dims, ((), ())), preferred_element_type=F32)


def lanes(shape):
    return lax.broadcasted_iota(I32, shape, len(shape) - 1)


def subs(shape):
    return lax.broadcasted_iota(I32, shape, len(shape) - 2)


def one_hot(mask):
    return jnp.where(mask, 1.0, 0.0).astype(BF16)


def call(kernel, outs, *args, smem=(), scratch=(), vmem=16):
    return pl.pallas_call(
        kernel,
        out_shape=outs,
        in_specs=[
            pl.BlockSpec(memory_space=pltpu.SMEM if i in smem else pltpu.VMEM)
            for i in range(len(args))
        ],
        out_specs=jax.tree.map(lambda _: pl.BlockSpec(memory_space=pltpu.VMEM), outs),
        scratch_shapes=list(scratch),
        compiler_params=pltpu.CompilerParams(vmem_limit_bytes=vmem * 2**20),
    )(*args)


def struct(shape, dtype):
    return jax.ShapeDtypeStruct(shape, dtype)


def route_kernel(count_ref, row_ref, owner_ref, bag_ref, table_ref, send_ref, names_ref):
    eye = subs((SLOTS, SLOTS)) == lanes((SLOTS, SLOTS))

    def column(ref):
        return jnp.sum(jnp.where(eye, ref[...].astype(F32), 0.0), axis=1, keepdims=True)

    row, bag = column(row_ref), column(bag_ref)
    owner = column(owner_ref)
    live = subs((SLOTS, BLOCK)) < count_ref[0]
    hits = jnp.where((owner == lanes((SLOTS, BLOCK)).astype(F32)) & live, 1.0, 0.0)
    before = one_hot(subs((SLOTS, SLOTS)) > lanes((SLOTS, SLOTS)))
    earlier = dot(before, hits.astype(BF16), NN)
    place = jnp.sum(earlier * hits, axis=1, keepdims=True)
    alive = jnp.sum(hits, axis=1, keepdims=True)
    target = jnp.where(alive > 0.5, owner * CAP + place, -1.0)
    at = target == lanes((SLOTS, ROWS * CAP)).astype(F32)
    looked = dot(one_hot(row == lanes((SLOTS, 1024)).astype(F32)), table_ref[...], NN)
    both = jnp.concatenate(
        [looked.astype(BF16), jnp.broadcast_to(bag, (SLOTS, BLOCK)).astype(BF16)], axis=1
    )
    sent = dot(one_hot(at), both, TN)
    send_ref[...] = jnp.concatenate(
        [
            sent[:, :BLOCK].reshape(ROWS, CAP, BLOCK),
            sent[:, BLOCK:].reshape(ROWS, CAP, BLOCK),
        ],
        axis=1,
    ).astype(BF16)
    named = jnp.sum(jnp.where(at, row + 1.0, 0.0), axis=0, keepdims=True)
    high = jnp.floor(named * (1.0 / 32.0))
    low = named - 32.0 * high
    names_ref[...] = jnp.concatenate(
        [part[:, i * BLOCK : (i + 1) * BLOCK] for part in (high, low) for i in range(4)], axis=0
    )


def pool_kernel(got_ref, dense_ref, ids_ref, names_ref, out_ref):
    got = got_ref[...].astype(F32)
    data = got[:, :CAP].reshape(ROWS * CAP, BLOCK).astype(BF16)
    bags = got[:, CAP:].reshape(ROWS * CAP, BLOCK)
    hot = one_hot(bags == lanes((ROWS * CAP, BLOCK)).astype(F32))
    pooled = dot(hot, data, TN)[:BATCH].astype(BF16).astype(F32)
    eye = subs((BLOCK, BLOCK)) == lanes((BLOCK, BLOCK))
    bag_rows = [
        jnp.sum(jnp.where(eye, bags[i * BLOCK : (i + 1) * BLOCK], 0.0), axis=0, keepdims=True)
        for i in range(4)
    ]
    meta = jnp.concatenate(bag_rows + [names_ref[...], jnp.zeros((4, BLOCK), F32)], axis=0)
    part = jnp.concatenate([pooled, dense_ref[...].astype(F32)], axis=1)
    ids = ids_ref[...].astype(F32)
    for c in range(COLS):
        top = jnp.concatenate([part[:, c * SLICE : (c + 1) * SLICE], ids], axis=1)
        out_ref[c] = jnp.concatenate([top, meta], axis=0).astype(BF16)


def cross_kernel(
    got_ref, tables_ref, left_ref, right_ref, weight_ref, bias_ref, out_ref, x_ref, counts_ref
):
    ids = got_ref[:, :BATCH, SLICE:].astype(F32).reshape(HOST, SLICE)
    part = got_ref[:, :BATCH, :SLICE].astype(F32).reshape(HOST, SLICE)
    name = lanes((HOST, NAMES)).astype(F32)
    pieces = []
    for t in range(TABLES):
        count = jnp.zeros((HOST, NAMES), F32)
        for j in range(4):
            count += jnp.where(ids[:, 4 * t + j : 4 * t + j + 1] == name, 1.0, 0.0)
        low = count.astype(BF16)
        counts_ref[t] = low
        pieces.append(dot(low, tables_ref[t], NT))
        if t % 2:
            x_ref[:, (t // 2) * BLOCK : (t // 2 + 1) * BLOCK] = jnp.concatenate(
                pieces, axis=1
            ).astype(BF16)
            pieces = []
    x_ref[:, WIDE - BLOCK :] = jnp.concatenate(pieces + [part], axis=1).astype(BF16)
    low_rank = jnp.zeros((HOST, RANK), F32)
    back = jnp.zeros((HOST, RANK), F32)
    plain = jnp.zeros((HOST, 1), F32)
    for n in range(4):
        cols = slice(n * 256, (n + 1) * 256)
        x = x_ref[:, cols]
        weighted = x.astype(F32) * weight_ref[:, cols]
        low_rank += dot(x, left_ref[cols, :], NN)
        back += dot(weighted.astype(BF16), right_ref[:, cols], NT)
        plain += jnp.sum(weighted * (bias_ref[:, cols] + 1.0), axis=1, keepdims=True)
    high = plain.astype(BF16).astype(F32)
    lane = lanes((HOST, BLOCK))
    rest = jnp.where(lane == 0, high, jnp.where(lane == 1, plain - high, 0.0))
    out_ref[:, :, :RANK] = low_rank.astype(BF16).reshape(COLS, BATCH, RANK)
    out_ref[:, :, RANK : 2 * RANK] = back.astype(BF16).reshape(COLS, BATCH, RANK)
    out_ref[:, :, 2 * RANK :] = rest.astype(BF16).reshape(COLS, BATCH, BLOCK)


def residue_kernel(got_ref, label_ref, out_ref):
    total = got_ref[0].astype(F32)
    for c in range(1, COLS):
        total += got_ref[c].astype(F32)
    low_rank = total[:, :RANK].astype(BF16).astype(F32)
    back = total[:, RANK : 2 * RANK]
    plain = total[:, 2 * RANK : 2 * RANK + 1] + total[:, 2 * RANK + 1 : 2 * RANK + 2]
    logits = jnp.sum(low_rank * back, axis=1, keepdims=True) + plain
    residue = (jax.nn.sigmoid(logits) - label_ref[...].astype(F32)) * LOSS_SCALE
    high = residue.astype(BF16).astype(F32)
    lane = lanes((BATCH, BLOCK))
    rest = jnp.where(lane == 0, high, jnp.where(lane == 1, residue - high, 0.0))
    block = jnp.concatenate([low_rank, residue * back, rest], axis=1).astype(BF16)
    for c in range(COLS):
        out_ref[c] = block


def part_kernel(got_ref, x_ref, left_ref, right_ref, weight_ref, bias_ref, out_ref):
    last = slice(WIDE - BLOCK, WIDE)
    low_rank = got_ref[:, :, :RANK].reshape(HOST, RANK)
    grad_rank = got_ref[:, :, RANK : 2 * RANK].reshape(HOST, RANK)
    rest = got_ref[:, :, 2 * RANK :].astype(F32).reshape(HOST, BLOCK)
    residue = rest[:, 0:1] + rest[:, 1:2]
    expanded = dot(low_rank, right_ref[:, last], NN) + bias_ref[:, last]
    grad = residue * weight_ref[:, last] * (expanded + 1.0) + dot(grad_rank, left_ref[last, :], NT)
    grad = grad[:, SLICE:].astype(BF16).astype(F32)
    blank = jnp.zeros((BATCH, SLICE), F32)
    for c in range(COLS):
        k = (c % 4) * 16
        own = jnp.concatenate([grad[c * BATCH : (c + 1) * BATCH], blank], axis=1)
        bag = jnp.concatenate(
            [grad[i * BATCH : (i + 1) * BATCH, k : k + 16] for i in range(COLS)], axis=1
        )
        out_ref[c] = jnp.concatenate([own, bag], axis=0).astype(BF16)


def grads_kernel(
    place_ref,
    got_ref,
    part_ref,
    meta_ref,
    x_ref,
    counts_ref,
    left_ref,
    right_ref,
    weight_ref,
    bias_ref,
    out_ref,
    sample_ref,
    right_scr,
):
    odd = place_ref[0]
    low_rank = got_ref[:, :, :RANK].reshape(HOST, RANK)
    grad_rank = got_ref[:, :, RANK : 2 * RANK].reshape(HOST, RANK)
    rest = got_ref[:, :, 2 * RANK :].astype(F32).reshape(HOST, BLOCK)
    residue = rest[:, 0:1] + rest[:, 1:2]

    def at(r):
        z, y = r // SIDE, r % SIDE
        return jnp.where(odd == 1, z, y), jnp.where(odd == 1, y, z)

    biases, tops = [], []
    for n in range(4):
        cols = slice(n * 256, (n + 1) * 256)
        x = x_ref[:, cols]
        wide = x.astype(F32)
        expanded = dot(low_rank, right_ref[:, cols], NN) + bias_ref[:, cols]
        tops.append(jnp.sum(residue * (wide * expanded + wide), axis=0, keepdims=True))
        grad_crossed = residue * weight_ref[:, cols]
        grad_expanded = grad_crossed * wide
        biases.append(jnp.sum(grad_expanded, axis=0, keepdims=True))
        right_scr[:, cols] = dot(low_rank, grad_expanded.astype(BF16), TN)
        left = dot(x, grad_rank, TN).astype(BF16)
        grad = grad_crossed * (expanded + 1.0) + dot(grad_rank, left_ref[cols, :], NT)
        grad = grad.astype(BF16)
        for i in range(16):
            a, b = at(16 * n + i)
            out_ref[a, b, :, :RANK] = left[16 * i : 16 * i + 16]
        for i in range(4):
            t = 4 * n + i
            if t < TABLES:
                medium = dot(grad[:, i * SLICE : (i + 1) * SLICE], counts_ref[t], TN).astype(BF16)
            else:
                medium = jnp.zeros((SLICE, NAMES), BF16)
            for k in range(4):
                a, b = at(4 * t + k)
                out_ref[a, b, :, 2 * RANK : 2 * RANK + NAMES] = medium[16 * k : 16 * k + 16]
    for r in range(ROWS):
        a, b = at(r)
        band = right_scr[8 * r : 8 * r + 8, :]
        out_ref[a, b, :, RANK : 2 * RANK] = jnp.concatenate(
            [band[:, :RANK], band[:, RANK:]], axis=0
        ).astype(BF16)

    bags = [
        jnp.concatenate(
            [meta_ref[c, BATCH : BATCH + 16, :].astype(F32)[i : i + 1] for i in range(4)], axis=1
        )
        for c in range(COLS)
    ]
    bag = subs((BATCH, ROWS * CAP)).astype(F32)
    hot = jnp.concatenate([jnp.where(b == bag, 1.0, 0.0) for b in bags], axis=0).astype(BF16)
    own = jnp.where(
        place_ref[1] == 1,
        part_ref[1, BATCH:, :].astype(F32),
        part_ref[0, BATCH:, :].astype(F32),
    )
    spread = jnp.concatenate([own] * COLS, axis=0)
    spread = jnp.where(
        subs((HOST, BLOCK)) // BATCH == lanes((HOST, BLOCK)) // 16, spread, 0.0
    ).astype(BF16)
    back = dot(hot, spread, TN).reshape(ROWS, CAP, BLOCK)
    back = jnp.concatenate([back[:, :, :SLICE], back[:, :, SLICE:]], axis=1)

    bias = jnp.concatenate(biases, axis=1)
    top = jnp.concatenate(tops, axis=1)
    blank = jnp.zeros((12, SLICE), F32)
    vectors = []
    for b in range(SIDE):
        pieces = [
            v[:, b * BLOCK + h * SLICE : b * BLOCK + (h + 1) * SLICE]
            for v in (bias, top)
            for h in range(2)
        ]
        vectors.append(jnp.concatenate(pieces + [blank], axis=0))
    vectors = jnp.stack(vectors, axis=0)
    out_ref[:, :, :, 2 * RANK + NAMES : 2 * RANK + NAMES + SLICE] = jnp.broadcast_to(
        vectors[None], (SIDE, SIDE, 16, SLICE)
    ).astype(BF16)
    low = back.astype(BF16)
    for r in range(ROWS):
        a, b = at(r)
        out_ref[a, b, :, 2 * RANK + NAMES + SLICE :] = low[r]
    sample_ref[...] = jnp.concatenate(
        [part_ref[c, :BATCH, :SLICE].astype(F32) for c in range(COLS)], axis=1
    ).astype(BF16)


SUMS = 2 * RANK + NAMES


def middle_kernel(got_ref, out_ref):
    vectors = []
    for b in range(SIDE):
        total = got_ref[0, b].astype(F32)
        for a in range(1, SIDE):
            total += got_ref[a, b].astype(F32)
        out_ref[b, :, :SUMS] = total[:, :SUMS].astype(BF16)
        vectors.append(total[:4, SUMS : SUMS + SLICE])
        for a in range(0, SIDE, 2):
            pair = [got_ref[a + i, b, :, SUMS + SLICE :].astype(F32) for i in range(2)]
            at = SUMS + a * SLICE
            out_ref[b, :, at : at + BLOCK] = jnp.concatenate(pair, axis=1).astype(BF16)
    packed = jnp.concatenate(
        [jnp.concatenate(vectors[:4], axis=0), jnp.concatenate(vectors[4:], axis=0)], axis=1
    ).astype(BF16)
    for b in range(SIDE):
        out_ref[b, :, SUMS + 512 :] = packed


def last_kernel(got_ref, left_ref, right_ref, bias_ref, top_ref, medium_ref):
    sums = got_ref[0, :, :SUMS].astype(F32)
    packed = got_ref[0, :, SUMS + 512 :].astype(F32)
    for a in range(1, SIDE):
        sums += got_ref[a, :, :SUMS].astype(F32)
        packed += got_ref[a, :, SUMS + 512 :].astype(F32)
    medium = sums[:, 2 * RANK :].astype(BF16)
    for r in range(ROWS):
        medium_ref[r] = medium
    left_ref[...] = sums[:, :RANK]
    right = sums[:, RANK : 2 * RANK]
    right_ref[...] = jnp.concatenate([right[:8], right[8:]], axis=1)
    for v, ref in ((0, bias_ref), (2, top_ref)):
        pieces = []
        for b in range(SIDE):
            at = (b // 4) * SLICE
            for h in range(2):
                i = 4 * (b % 4) + v + h
                pieces.append(packed[i : i + 1, at : at + SLICE])
        ref[...] = jnp.concatenate(pieces, axis=1)


def rows_kernel(place_ref, got_ref, meta_ref, out_ref, data_scr):
    odd = place_ref[0]
    for second in range(SIDE):
        for first in range(SIDE):
            at = SUMS + first * SLICE
            block = got_ref[second, :, at : at + SLICE].astype(F32)
            r = jnp.where(odd == 1, first * SIDE + second, second * SIDE + first)
            data_scr[r] = jnp.concatenate([block[:CAP], block[CAP:]], axis=1)
    data = data_scr[...].reshape(ROWS * CAP, BLOCK)
    group = lanes((ROWS * CAP, BLOCK)) // 16
    row = subs((1024, ROWS * CAP)).astype(F32) + 1.0
    total = jnp.zeros((1024, BLOCK), F32)
    for c in range(COLS):
        meta = meta_ref[c, BATCH : BATCH + 16, :].astype(F32)
        name = jnp.concatenate(
            [meta[4 + i : 5 + i] * 32.0 + meta[8 + i : 9 + i] for i in range(4)], axis=1
        )
        total += dot(one_hot(name == row), jnp.where(group == c, data, 0.0).astype(BF16), NN)
    for shift in (64, 32, 16):
        total = total + pltpu.roll(total, shift, 1)
    slot = lanes((BLOCK, BLOCK)) // 16
    packed = jnp.zeros((BLOCK, BLOCK), F32)
    for i in range(8):
        packed = jnp.where(slot == i, total[i * BLOCK : (i + 1) * BLOCK], packed)
    out_ref[0] = packed.astype(BF16)


def giant_kernel(got_ref, out_ref):
    slot = lanes((BLOCK, BLOCK)) // 16
    for i in range(8):
        block = jnp.zeros((BLOCK, BLOCK), F32)
        for c in range(COLS):
            piece = got_ref[c].astype(F32)
            shift = ((c - i) * 16) % BLOCK
            if shift:
                piece = pltpu.roll(piece, shift, 1)
            block = jnp.where(slot == c, piece, block)
        out_ref[i * BLOCK : (i + 1) * BLOCK, :] = block


def medium_kernel(got_ref, out_ref):
    for t in range(TABLES):
        block = got_ref[4 * t : 4 * t + 4].astype(F32).reshape(SLICE, NAMES)
        out_ref[t] = block


def sides():
    first, second = [], []
    for c in range(COLS):
        for k in range(SIDE):
            along_y = [(k * SIDE + y) * COLS + c for y in range(SIDE)]
            along_z = [(z * SIDE + k) * COLS + c for z in range(SIDE)]
            first.append(along_z if c % 2 else along_y)
            second.append(along_y if c % 2 else along_z)
    return first, second


def swap(value, axis, groups=None):
    return lax.all_to_all(
        value, axis, split_axis=0, concat_axis=0, tiled=True, axis_index_groups=groups
    )


def body(
    giant_table,
    look_row,
    look_owner,
    look_bag,
    look_count,
    medium_tables,
    medium_ids,
    medium_lengths,
    dense_features,
    click_labels,
    cross_left,
    cross_right,
    cross_bias,
    top_weight,
):
    first, second = sides()
    col = lax.axis_index("col")
    place = jnp.stack([col % 2, col // 4]).astype(I32)
    bias, weight = cross_bias.reshape(1, WIDE), top_weight.reshape(1, WIDE)
    live = jnp.arange(4)[None, None, :] < medium_lengths[:, :, None]
    ids = jnp.where(live, medium_ids, NAMES).reshape(BATCH, 4 * TABLES).astype(BF16)
    ids = jnp.pad(ids, ((0, 0), (0, SLICE - 4 * TABLES)))

    send, names = call(
        route_kernel,
        (struct((ROWS, 2 * CAP, BLOCK), BF16), struct((8, BLOCK), F32)),
        look_count,
        look_row.reshape(1, SLOTS),
        look_owner.reshape(1, SLOTS),
        look_bag.reshape(1, SLOTS),
        giant_table,
        smem=(0,),
        vmem=60,
    )
    got = swap(send, "row")
    send = call(
        pool_kernel, struct((COLS, 48, BLOCK), BF16), got, dense_features, ids, names
    )
    meta = swap(send, "col")
    send, x, counts = call(
        cross_kernel,
        (
            struct((COLS, BATCH, 2 * RANK + BLOCK), BF16),
            struct((HOST, WIDE), BF16),
            struct((TABLES, HOST, NAMES), BF16),
        ),
        meta,
        jnp.swapaxes(medium_tables, 1, 2),
        cross_left,
        cross_right,
        weight,
        bias,
    )
    got = swap(send, "col")
    send = call(
        residue_kernel,
        struct((COLS, BATCH, 2 * RANK + BLOCK), BF16),
        got,
        click_labels.reshape(BATCH, 1),
    )
    ranks = swap(send, "col")
    send = call(
        part_kernel,
        struct((COLS, 2 * BATCH, BLOCK), BF16),
        ranks,
        x,
        cross_left,
        cross_right,
        weight,
        bias,
    )
    parts = swap(send, "col")
    send, sample_grads = call(
        grads_kernel,
        (
            struct((SIDE, SIDE, 16, SUMS + BLOCK), BF16),
            struct((BATCH, COLS * SLICE), BF16),
        ),
        place,
        ranks,
        parts,
        meta,
        x,
        counts,
        cross_left,
        cross_right,
        weight,
        bias,
        smem=(0,),
        scratch=(pltpu.VMEM((RANK, WIDE), F32),),
        vmem=24,
    )
    got = swap(send, ("row", "col"), first)
    send = call(middle_kernel, struct((SIDE, 16, SUMS + 512 + BLOCK), BF16), got)
    got = swap(send, ("row", "col"), second)
    left_grad, right_grad, bias_grad, top_grad, medium = call(
        last_kernel,
        (
            struct((16, RANK), F32),
            struct((8, WIDE), F32),
            struct((1, WIDE), F32),
            struct((1, WIDE), F32),
            struct((ROWS, 16, NAMES), BF16),
        ),
        got,
    )
    medium = swap(medium, "row")
    giant = call(
        rows_kernel,
        struct((1, BLOCK, BLOCK), BF16),
        place,
        got,
        meta,
        smem=(0,),
        scratch=(pltpu.VMEM((ROWS, CAP, BLOCK), F32),),
    )
    giant_grad = call(
        giant_kernel,
        struct((1024, BLOCK), F32),
        lax.all_gather(giant, "col", axis=0, tiled=True),
    )
    medium_grad = jnp.swapaxes(
        call(medium_kernel, struct((TABLES, SLICE, NAMES), F32), medium), 1, 2
    )
    return (
        sample_grads,
        giant_grad,
        medium_grad,
        left_grad,
        right_grad,
        bias_grad.reshape(WIDE),
        top_grad.reshape(WIDE),
    )


def solution(mesh):
    both = P(("row", "col"))
    placed = (
        P("row", None),
        both,
        P(("row", "col"), None),
        both,
        both,
        P(None, None, "col"),
        P(("row", "col"), None, None),
        P(("row", "col"), None),
        P(("row", "col"), None),
        both,
        P("col", None),
        P(None, "col"),
        P("col"),
        P("col"),
    )
    return jax.shard_map(
        body,
        mesh=mesh,
        in_specs=placed,
        out_specs=(
            P(("row", "col"), None),
            P("row", None),
            P(None, None, "col"),
            P(("col", "row"), None),
            P("row", "col"),
            P("col"),
            P("col"),
        ),
        check_vma=False,
    )
```

```python
import functools

import jax
import jax.numpy as jnp
from jax import lax
from jax.experimental import pallas as pl
from jax.experimental.pallas import tpu as pltpu
from jax.sharding import PartitionSpec as P

LOSS_SCALE = 0.015625

F32, BF16, I32 = jnp.float32, jnp.bfloat16, jnp.int32
ROWS, COLS = 64, 8
SIDE = 8
BATCH, HOST = 32, 256
SLOTS, CAP = 256, 8
WIDE, RANK = 1024, 512
TABLES, NAMES, SLICE = 15, 256, 64
BLOCK = 128

NN = ((1,), (0,))
NT = ((1,), (1,))
TN = ((0,), (0,))


def dot(left, right, dims):
    return lax.dot_general(left, right, (dims, ((), ())), preferred_element_type=F32)


def lanes(shape):
    return lax.broadcasted_iota(I32, shape, len(shape) - 1)


def subs(shape):
    return lax.broadcasted_iota(I32, shape, len(shape) - 2)


def one_hot(mask):
    return jnp.where(mask, 1.0, 0.0).astype(BF16)


def call(
    kernel,
    outs,
    *args,
    smem=(),
    far=(),
    far_outs=(),
    scratch=(),
    copies=0,
    vmem=16,
    alias=None,
    cost=None,
):
    single = not isinstance(outs, tuple)
    specs = tuple(
        pl.BlockSpec(memory_space=pltpu.HBM if i in far_outs else pltpu.VMEM)
        for i in range(1 if single else len(outs))
    )
    return pl.pallas_call(
        kernel,
        out_shape=outs,
        in_specs=[
            pl.BlockSpec(
                memory_space=pltpu.SMEM if i in smem else pltpu.HBM if i in far else pltpu.VMEM
            )
            for i in range(len(args))
        ],
        out_specs=specs[0] if single else specs,
        scratch_shapes=[*scratch, *[pltpu.SemaphoreType.DMA] * copies],
        input_output_aliases=alias or {},
        cost_estimate=cost,
        compiler_params=pltpu.CompilerParams(vmem_limit_bytes=vmem * 2**20),
    )(*args)


def begin(*triples):
    copies = [pltpu.make_async_copy(*triple) for triple in triples]
    for copy in copies:
        copy.start()
    return copies


def struct(shape, dtype):
    return jax.ShapeDtypeStruct(shape, dtype)


def route_kernel(count_ref, row_ref, owner_ref, bag_ref, table_ref, send_ref, at_ref):
    eye = subs((SLOTS, SLOTS)) == lanes((SLOTS, SLOTS))

    def column(ref):
        return jnp.sum(jnp.where(eye, ref[...].astype(F32), 0.0), axis=1, keepdims=True)

    row, bag = column(row_ref), column(bag_ref)
    owner = column(owner_ref)
    live = subs((SLOTS, BLOCK)) < count_ref[0]
    hits = jnp.where((owner == lanes((SLOTS, BLOCK)).astype(F32)) & live, 1.0, 0.0)
    before = one_hot(subs((SLOTS, SLOTS)) > lanes((SLOTS, SLOTS)))
    earlier = dot(before, hits.astype(BF16), NN)
    place = jnp.sum(earlier * hits, axis=1, keepdims=True)
    alive = jnp.sum(hits, axis=1, keepdims=True)
    target = jnp.where(alive > 0.5, owner * CAP + place, -1.0)
    at = one_hot(target == lanes((SLOTS, ROWS * CAP)).astype(F32))
    at_ref[...] = at
    looked = dot(one_hot(row == lanes((SLOTS, 1024)).astype(F32)), table_ref[...], NN)
    both = jnp.concatenate(
        [looked.astype(BF16), jnp.broadcast_to(bag, (SLOTS, BLOCK)).astype(BF16)], axis=1
    )
    sent = dot(at, both, TN)
    send_ref[...] = jnp.concatenate(
        [
            sent[:, :BLOCK].reshape(ROWS, CAP, BLOCK),
            sent[:, BLOCK:].reshape(ROWS, CAP, BLOCK),
        ],
        axis=1,
    ).astype(BF16)


def pool_kernel(got_ref, dense_ref, ids_ref, row_ref, out_ref, hot_ref):
    got = got_ref[...].astype(F32)
    data = got[:, :CAP].reshape(ROWS * CAP, BLOCK).astype(BF16)
    bags = got[:, CAP:].reshape(ROWS * CAP, BLOCK)
    hot = one_hot(bags == lanes((ROWS * CAP, BLOCK)).astype(F32))
    hot_ref[...] = hot
    pooled = dot(hot, data, TN)[:BATCH].astype(BF16).astype(F32)
    row = row_ref[...].astype(F32)
    high = jnp.floor(row * (1.0 / 32.0))
    low = row - 32.0 * high
    meta = [part[:, i * BLOCK : (i + 1) * BLOCK] for part in (high, low) for i in range(2)]
    meta = jnp.concatenate(meta + [jnp.zeros((12, BLOCK), F32)], axis=0)
    part = jnp.concatenate([pooled, dense_ref[...].astype(F32)], axis=1)
    ids = ids_ref[...].astype(F32)
    for c in range(COLS):
        top = jnp.concatenate([part[:, c * SLICE : (c + 1) * SLICE], ids], axis=1)
        out_ref[c] = jnp.concatenate([top, meta], axis=0).astype(BF16)


def cross_kernel(
    got_ref,
    tables_far,
    left_far,
    right_far,
    weight_far,
    bias_far,
    out_far,
    x_far,
    counts_far,
    left_end_ref,
    right_end_ref,
    ends_ref,
    tables_ref,
    left_ref,
    right_ref,
    weight_ref,
    bias_ref,
    out_ref,
    x_ref,
    counts_ref,
    *sems,
):
    tables_in, weight_in, bias_in, left_in, right_in = begin(
        (tables_far, tables_ref, sems[0]),
        (weight_far, weight_ref, sems[1]),
        (bias_far, bias_ref, sems[2]),
        (left_far, left_ref, sems[3]),
        (right_far, right_ref, sems[4]),
    )
    ids = got_ref[:, :BATCH, SLICE:].astype(F32).reshape(HOST, SLICE)
    part = got_ref[:, :BATCH, :SLICE].astype(F32).reshape(HOST, SLICE)
    name = lanes((HOST, NAMES)).astype(F32)
    for t in range(TABLES):
        count = jnp.zeros((HOST, NAMES), F32)
        for j in range(4):
            count += jnp.where(ids[:, 4 * t + j : 4 * t + j + 1] == name, 1.0, 0.0)
        counts_ref[t] = count.astype(BF16)
    (counts_out,) = begin((counts_ref, counts_far, sems[5]))
    tables_in.wait()
    pieces = []
    for t in range(TABLES):
        pieces.append(dot(counts_ref[t], tables_ref[t], NT))
        if t % 2:
            x_ref[:, (t // 2) * BLOCK : (t // 2 + 1) * BLOCK] = jnp.concatenate(
                pieces, axis=1
            ).astype(BF16)
            pieces = []
    x_ref[:, WIDE - BLOCK :] = jnp.concatenate(pieces + [part], axis=1).astype(BF16)
    (x_out,) = begin((x_ref, x_far, sems[6]))
    for copy in (weight_in, bias_in, left_in, right_in):
        copy.wait()
    low_rank = jnp.zeros((HOST, RANK), F32)
    back = jnp.zeros((HOST, RANK), F32)
    plain = jnp.zeros((HOST, 1), F32)
    for n in range(4):
        cols = slice(n * 256, (n + 1) * 256)
        x = x_ref[:, cols]
        weighted = x.astype(F32) * weight_ref[:, cols]
        low_rank += dot(x, left_ref[cols, :], NN)
        back += dot(weighted.astype(BF16), right_ref[:, cols], NT)
        plain += jnp.sum(weighted * (bias_ref[:, cols] + 1.0), axis=1, keepdims=True)
    high = plain.astype(BF16).astype(F32)
    lane = lanes((HOST, BLOCK))
    rest = jnp.where(lane == 0, high, jnp.where(lane == 1, plain - high, 0.0))
    out_ref[:, :, :RANK] = low_rank.astype(BF16).reshape(COLS, BATCH, RANK)
    out_ref[:, :, RANK : 2 * RANK] = back.astype(BF16).reshape(COLS, BATCH, RANK)
    out_ref[:, :, 2 * RANK :] = rest.astype(BF16).reshape(COLS, BATCH, BLOCK)
    (out_out,) = begin((out_ref, out_far, sems[7]))
    left_end_ref[...] = left_ref[WIDE - BLOCK :, :]
    right_end_ref[...] = right_ref[:, WIDE - BLOCK :]
    ends_ref[0:1, :] = weight_ref[:, WIDE - BLOCK :]
    ends_ref[1:2, :] = bias_ref[:, WIDE - BLOCK :]
    for copy in (counts_out, x_out, out_out):
        copy.wait()


def residue_kernel(got_ref, label_ref, out_ref):
    total = got_ref[0].astype(F32)
    for c in range(1, COLS):
        total += got_ref[c].astype(F32)
    low_rank = total[:, :RANK].astype(BF16).astype(F32)
    back = total[:, RANK : 2 * RANK]
    plain = total[:, 2 * RANK : 2 * RANK + 1] + total[:, 2 * RANK + 1 : 2 * RANK + 2]
    logits = jnp.sum(low_rank * back, axis=1, keepdims=True) + plain
    eye = subs((BATCH, BATCH)) == lanes((BATCH, BATCH))
    label = jnp.sum(jnp.where(eye, label_ref[...].astype(F32), 0.0), axis=1, keepdims=True)
    residue = (jax.nn.sigmoid(logits) - label) * LOSS_SCALE
    high = residue.astype(BF16).astype(F32)
    lane = lanes((BATCH, BLOCK))
    rest = jnp.where(lane == 0, high, jnp.where(lane == 1, residue - high, 0.0))
    block = jnp.concatenate([low_rank, residue * back, rest], axis=1).astype(BF16)
    for c in range(COLS):
        out_ref[c] = block


def part_kernel(got_ref, left_ref, right_ref, ends_ref, out_far, out_ref, out_sem):
    low_rank = got_ref[:, :, :RANK].reshape(HOST, RANK)
    grad_rank = got_ref[:, :, RANK : 2 * RANK].reshape(HOST, RANK)
    rest = got_ref[:, :, 2 * RANK :].astype(F32).reshape(HOST, BLOCK)
    residue = rest[:, 0:1] + rest[:, 1:2]
    expanded = dot(low_rank, right_ref[...], NN) + ends_ref[1:2, :]
    grad = residue * ends_ref[0:1, :] * (expanded + 1.0) + dot(grad_rank, left_ref[...], NT)
    out_ref[...] = grad.astype(BF16).reshape(COLS, BATCH, BLOCK)
    (copy,) = begin((out_ref, out_far, out_sem))
    copy.wait()


def order(odd, r):
    z, y = r // SIDE, r % SIDE
    return jnp.where(odd == 1, z, y), jnp.where(odd == 1, y, z)


def grads_kernel(
    got_far,
    x_far,
    counts_far,
    left_far,
    right_far,
    weight_far,
    bias_far,
    out_ref,
    vector_ref,
    got_ref,
    x_ref,
    counts_ref,
    left_ref,
    right_ref,
    weight_ref,
    bias_ref,
    band_ref,
    grad_ref,
    *sems,
):
    got_in, right_in, x_in, weight_in, bias_in = begin(
        (got_far, got_ref, sems[0]),
        (right_far, right_ref, sems[1]),
        (x_far, x_ref, sems[2]),
        (weight_far, weight_ref, sems[3]),
        (bias_far, bias_ref, sems[4]),
    )
    odd = lax.axis_index("col") % 2
    for copy in (got_in, right_in, x_in, weight_in, bias_in):
        copy.wait()
    left_in, counts_in = begin(
        (left_far, left_ref, sems[5]),
        (counts_far, counts_ref, sems[6]),
    )
    low_rank = got_ref[:, :, :RANK].reshape(HOST, RANK)
    grad_rank = got_ref[:, :, RANK : 2 * RANK].reshape(HOST, RANK)
    rest = got_ref[:, :, 2 * RANK :].astype(F32).reshape(HOST, BLOCK)
    residue = rest[:, 0:1] + rest[:, 1:2]
    for n in range(4):
        cols = slice(n * 256, (n + 1) * 256)
        x = x_ref[:, cols]
        wide = x.astype(F32)
        expanded = dot(low_rank, right_ref[:, cols], NN) + bias_ref[:, cols]
        vector_ref[1:2, cols] = jnp.sum(
            residue * (wide * expanded + wide), axis=0, keepdims=True
        )
        grad_crossed = residue * weight_ref[:, cols]
        grad_expanded = grad_crossed * wide
        vector_ref[0:1, cols] = jnp.sum(grad_expanded, axis=0, keepdims=True)
        grad_ref[:, cols] = grad_crossed * (expanded + 1.0)
        band_ref[:, cols] = dot(low_rank, grad_expanded.astype(BF16), TN)
        left = dot(x, grad_rank, TN).astype(BF16)
        for i in range(16):
            a, b = order(odd, 16 * n + i)
            out_ref[a, b, :, :RANK] = left[16 * i : 16 * i + 16]
    for r in range(ROWS):
        a, b = order(odd, r)
        band = band_ref[8 * r : 8 * r + 8, :]
        out_ref[a, b, :, RANK : 2 * RANK] = jnp.concatenate(
            [band[:, :RANK], band[:, RANK:]], axis=0
        ).astype(BF16)
    left_in.wait()
    counts_in.wait()
    for n in range(4):
        cols = slice(n * 256, (n + 1) * 256)
        grad = grad_ref[:, cols] + dot(grad_rank, left_ref[cols, :], NT)
        grad = grad.astype(BF16)
        for i in range(4):
            t = 4 * n + i
            if t < TABLES:
                medium = dot(grad[:, i * SLICE : (i + 1) * SLICE], counts_ref[t], TN).astype(BF16)
            else:
                medium = jnp.zeros((SLICE, NAMES), BF16)
            for k in range(4):
                a, b = order(odd, 4 * t + k)
                out_ref[a, b, :, 2 * RANK : SUMS] = medium[16 * k : 16 * k + 16]

def back_kernel(part_ref, hot_ref, vector_ref, _, out_far, sample_ref, out_ref, out_sem):
    odd = lax.axis_index("col") % 2
    grads = jnp.concatenate(
        [part_ref[c].astype(F32)[:, SLICE:] for c in range(COLS)], axis=1
    )
    sample_ref[...] = grads.astype(BF16)
    bag = jnp.concatenate([grads[:, :BLOCK], jnp.zeros((BLOCK - BATCH, BLOCK), F32)], axis=0)
    back = dot(hot_ref[...], bag.astype(BF16), NN).reshape(ROWS, CAP, BLOCK)
    back = jnp.concatenate([back[:, :, :SLICE], back[:, :, SLICE:]], axis=1)
    back = jnp.concatenate([back, back], axis=2)
    blank = jnp.zeros((12, SLICE), F32)
    vectors = []
    for b in range(SIDE):
        pieces = [
            vector_ref[v : v + 1, b * BLOCK + h * SLICE : b * BLOCK + (h + 1) * SLICE]
            for v in range(2)
            for h in range(2)
        ]
        vector = jnp.concatenate(pieces + [blank], axis=0)
        vectors.append(jnp.concatenate([vector, vector], axis=1))
    first = lanes((16, BLOCK)) < SLICE
    for r in range(ROWS):
        a, b = order(odd, r)
        vector = jnp.where(odd == 1, vectors[r % SIDE], vectors[r // SIDE])
        out_ref[a, b] = jnp.where(first, vector, back[r]).astype(BF16)
    (copy,) = begin((out_ref, out_far.at[:, :, :, SUMS:], out_sem))
    copy.wait()


SUMS = 2 * RANK + NAMES


def middle_kernel(got_ref, out_ref):
    vectors = []
    for b in range(SIDE):
        total = got_ref[0, b].astype(F32)
        for a in range(1, SIDE):
            total += got_ref[a, b].astype(F32)
        out_ref[b, :, :SUMS] = total[:, :SUMS].astype(BF16)
        vectors.append(total[:4, SUMS : SUMS + SLICE])
        for a in range(0, SIDE, 2):
            pair = [got_ref[a + i, b, :, SUMS + SLICE :].astype(F32) for i in range(2)]
            at = SUMS + a * SLICE
            out_ref[b, :, at : at + BLOCK] = jnp.concatenate(pair, axis=1).astype(BF16)
    packed = jnp.concatenate(
        [jnp.concatenate(vectors[:4], axis=0), jnp.concatenate(vectors[4:], axis=0)], axis=1
    ).astype(BF16)
    for b in range(SIDE):
        out_ref[b, :, SUMS + 512 :] = packed


def last_kernel(got_ref, left_ref, right_ref, bias_ref, top_ref, medium_ref):
    sums = got_ref[0, :, :SUMS].astype(F32)
    packed = got_ref[0, :, SUMS + 512 :].astype(F32)
    for a in range(1, SIDE):
        sums += got_ref[a, :, :SUMS].astype(F32)
        packed += got_ref[a, :, SUMS + 512 :].astype(F32)
    medium = sums[:, 2 * RANK :].astype(BF16)
    for r in range(ROWS):
        medium_ref[r] = medium
    left_ref[...] = sums[:, :RANK]
    right = sums[:, RANK : 2 * RANK]
    right_ref[...] = jnp.concatenate([right[:8], right[8:]], axis=1)
    for v, ref in ((0, bias_ref), (2, top_ref)):
        pieces = []
        for b in range(SIDE):
            at = (b // 4) * SLICE
            for h in range(2):
                i = 4 * (b % 4) + v + h
                pieces.append(packed[i : i + 1, at : at + SLICE])
        ref[...] = jnp.concatenate(pieces, axis=1)


def slots_kernel(got_ref, at_ref, out_ref, data_scr):
    odd = lax.axis_index("col") % 2
    for second in range(SIDE):
        for first in range(SIDE):
            at = SUMS + first * SLICE
            block = got_ref[second, :, at : at + SLICE].astype(F32)
            r = jnp.where(odd == 1, first * SIDE + second, second * SIDE + first)
            data_scr[r] = jnp.concatenate([block[:CAP], block[CAP:]], axis=1)
    data = data_scr[...].reshape(ROWS * CAP, BLOCK).astype(BF16)
    out_ref[0] = dot(at_ref[...], data, NN).astype(BF16)


def giant_kernel(got_ref, meta_ref, out_ref):
    row = subs((1024, SLOTS)).astype(F32)
    total = jnp.zeros((1024, BLOCK), F32)
    for c in range(COLS):
        meta = meta_ref[c, BATCH : BATCH + 16, :].astype(F32)
        name = jnp.concatenate(
            [meta[i : i + 1] * 32.0 + meta[2 + i : 3 + i] for i in range(2)], axis=1
        )
        total += dot(one_hot(name == row), got_ref[c], NN)
    out_ref[...] = total


def medium_kernel(got_ref, out_ref):
    for t in range(TABLES):
        block = got_ref[4 * t : 4 * t + 4].astype(F32).reshape(SLICE, NAMES)
        out_ref[t] = block


def sides():
    first, second = [], []
    for c in range(COLS):
        for k in range(SIDE):
            along_y = [(k * SIDE + y) * COLS + c for y in range(SIDE)]
            along_z = [(z * SIDE + k) * COLS + c for z in range(SIDE)]
            first.append(along_z if c % 2 else along_y)
            second.append(along_y if c % 2 else along_z)
    return first, second


def swap(value, axis, groups=None):
    return lax.all_to_all(
        value, axis, split_axis=0, concat_axis=0, tiled=True, axis_index_groups=groups
    )


def body(
    giant_table,
    look_row,
    look_owner,
    look_bag,
    look_count,
    medium_tables,
    medium_ids,
    medium_lengths,
    dense_features,
    click_labels,
    cross_left,
    cross_right,
    cross_bias,
    top_weight,
):
    first, second = sides()
    bias, weight = cross_bias.reshape(1, WIDE), top_weight.reshape(1, WIDE)
    live = jnp.arange(4)[None, None, :] < medium_lengths[:, :, None]
    ids = jnp.where(live, medium_ids, NAMES).reshape(BATCH, 4 * TABLES).astype(BF16)
    ids = jnp.pad(ids, ((0, 0), (0, SLICE - 4 * TABLES)))

    look_row = look_row.reshape(1, SLOTS)
    send, at = call(
        route_kernel,
        (struct((ROWS, 2 * CAP, BLOCK), BF16), struct((SLOTS, ROWS * CAP), BF16)),
        look_count,
        look_row,
        look_owner.reshape(1, SLOTS),
        look_bag.reshape(1, SLOTS),
        giant_table,
        smem=(0,),
        vmem=60,
    )
    got = swap(send, "row")
    send, hot = call(
        pool_kernel,
        (struct((COLS, 48, BLOCK), BF16), struct((ROWS * CAP, BLOCK), BF16)),
        got,
        dense_features,
        ids,
        look_row,
    )
    meta = swap(send, "col")
    send, x, counts, left_end, right_end, ends = call(
        cross_kernel,
        (
            struct((COLS, BATCH, 2 * RANK + BLOCK), BF16),
            struct((HOST, WIDE), BF16),
            struct((TABLES, HOST, NAMES), BF16),
            struct((BLOCK, RANK), BF16),
            struct((RANK, BLOCK), BF16),
            struct((2, BLOCK), F32),
        ),
        meta,
        jnp.swapaxes(medium_tables, 1, 2),
        cross_left,
        cross_right,
        weight,
        bias,
        far=(1, 2, 3, 4, 5),
        far_outs=(0, 1, 2),
        scratch=(
            pltpu.VMEM((TABLES, SLICE, NAMES), BF16),
            pltpu.VMEM((WIDE, RANK), BF16),
            pltpu.VMEM((RANK, WIDE), BF16),
            pltpu.VMEM((1, WIDE), F32),
            pltpu.VMEM((1, WIDE), F32),
            pltpu.VMEM((COLS, BATCH, 2 * RANK + BLOCK), BF16),
            pltpu.VMEM((HOST, WIDE), BF16),
            pltpu.VMEM((TABLES, HOST, NAMES), BF16),
        ),
        copies=8,
        vmem=60,
    )
    got = swap(send, "col")
    send = call(
        residue_kernel,
        struct((COLS, BATCH, 2 * RANK + BLOCK), BF16),
        got,
        click_labels.reshape(1, BATCH),
    )
    ranks = swap(send, "col")
    send = call(
        part_kernel,
        struct((COLS, BATCH, BLOCK), BF16),
        ranks,
        left_end,
        right_end,
        ends,
        far_outs=(0,),
        scratch=(pltpu.VMEM((COLS, BATCH, BLOCK), BF16),),
        copies=1,
    )
    parts = swap(send, "col")
    send, vectors = call(
        grads_kernel,
        (struct((SIDE, SIDE, 16, SUMS + BLOCK), BF16), struct((2, WIDE), F32)),
        ranks,
        x,
        counts,
        cross_left,
        cross_right,
        weight,
        bias,
        far=range(7),
        scratch=(
            pltpu.VMEM((COLS, BATCH, 2 * RANK + BLOCK), BF16),
            pltpu.VMEM((HOST, WIDE), BF16),
            pltpu.VMEM((TABLES, HOST, NAMES), BF16),
            pltpu.VMEM((WIDE, RANK), BF16),
            pltpu.VMEM((RANK, WIDE), BF16),
            pltpu.VMEM((1, WIDE), F32),
            pltpu.VMEM((1, WIDE), F32),
            pltpu.VMEM((RANK, WIDE), F32),
            pltpu.VMEM((HOST, WIDE), F32),
        ),
        copies=7,
        vmem=60,
        cost=pl.CostEstimate(flops=3 * 10**9, bytes_accessed=10**7, transcendentals=0),
    )
    send, sample_grads = call(
        back_kernel,
        (
            struct((SIDE, SIDE, 16, SUMS + BLOCK), BF16),
            struct((BATCH, COLS * SLICE), BF16),
        ),
        parts,
        hot,
        vectors,
        send,
        far=(3,),
        far_outs=(0,),
        scratch=(pltpu.VMEM((SIDE, SIDE, 16, BLOCK), BF16),),
        copies=1,
        alias={3: 0},
        vmem=60,
    )
    got = swap(send, ("row", "col"), first)
    send = call(middle_kernel, struct((SIDE, 16, SUMS + 512 + BLOCK), BF16), got)
    got = swap(send, ("row", "col"), second)
    left_grad, right_grad, bias_grad, top_grad, medium = call(
        last_kernel,
        (
            struct((16, RANK), F32),
            struct((8, WIDE), F32),
            struct((1, WIDE), F32),
            struct((1, WIDE), F32),
            struct((ROWS, 16, NAMES), BF16),
        ),
        got,
    )
    medium = swap(medium, "row")
    slots = call(
        slots_kernel,
        struct((1, SLOTS, BLOCK), BF16),
        got,
        at,
        scratch=(pltpu.VMEM((ROWS, CAP, BLOCK), F32),),
    )
    giant_grad = call(
        giant_kernel,
        struct((1024, BLOCK), F32),
        lax.all_gather(slots, "col", axis=0, tiled=True),
        meta,
    )
    medium_grad = jnp.swapaxes(
        call(medium_kernel, struct((TABLES, SLICE, NAMES), F32), medium), 1, 2
    )
    return (
        sample_grads,
        giant_grad,
        medium_grad,
        left_grad,
        right_grad,
        bias_grad.reshape(WIDE),
        top_grad.reshape(WIDE),
    )


def solution(mesh):
    both = P(("row", "col"))
    placed = (
        P("row", None),
        both,
        P(("row", "col"), None),
        both,
        both,
        P(None, None, "col"),
        P(("row", "col"), None, None),
        P(("row", "col"), None),
        P(("row", "col"), None),
        both,
        P("col", None),
        P(None, "col"),
        P("col"),
        P("col"),
    )
    return jax.shard_map(
        body,
        mesh=mesh,
        in_specs=placed,
        out_specs=(
            P(("row", "col"), None),
            P("row", None),
            P(None, None, "col"),
            P(("col", "row"), None),
            P("row", "col"),
            P("col"),
            P("col"),
        ),
        check_vma=False,
    )
```

```python
import functools

import jax
import jax.numpy as jnp
from jax import lax
from jax.experimental import pallas as pl
from jax.experimental.pallas import tpu as pltpu
from jax.sharding import PartitionSpec as P

LOSS_SCALE = 0.015625

F32, BF16, I32 = jnp.float32, jnp.bfloat16, jnp.int32
ROWS, COLS = 64, 8
SIDE = 8
BATCH, HOST = 32, 256
SLOTS, CAP = 256, 8
WIDE, RANK = 1024, 512
TABLES, NAMES, SLICE = 15, 256, 64
BLOCK = 128

NN = ((1,), (0,))
NT = ((1,), (1,))
TN = ((0,), (0,))


def dot(left, right, dims):
    return lax.dot_general(left, right, (dims, ((), ())), preferred_element_type=F32)


def lanes(shape):
    return lax.broadcasted_iota(I32, shape, len(shape) - 1)


def subs(shape):
    return lax.broadcasted_iota(I32, shape, len(shape) - 2)


def one_hot(mask):
    return jnp.where(mask, 1.0, 0.0).astype(BF16)


def call(
    kernel,
    outs,
    *args,
    smem=(),
    far=(),
    far_outs=(),
    scratch=(),
    copies=0,
    vmem=16,
    alias=None,
    cost=None,
    pinned=(),
    free=(),
    free_outs=(),
):
    single = not isinstance(outs, tuple)
    args = [
        pltpu.with_memory_space_constraint(arg, pltpu.HBM) if i in pinned else arg
        for i, arg in enumerate(args)
    ]
    specs = tuple(
        pl.BlockSpec(
            memory_space=pl.ANY
            if i in free_outs
            else pltpu.HBM
            if i in far_outs
            else pltpu.VMEM
        )
        for i in range(1 if single else len(outs))
    )
    return pl.pallas_call(
        kernel,
        out_shape=outs,
        in_specs=[
            pl.BlockSpec(
                memory_space=pltpu.SMEM
                if i in smem
                else pl.ANY
                if i in free
                else pltpu.HBM
                if i in far
                else pltpu.VMEM
            )
            for i in range(len(args))
        ],
        out_specs=specs[0] if single else specs,
        scratch_shapes=[*scratch, *[pltpu.SemaphoreType.DMA] * copies],
        input_output_aliases=alias or {},
        cost_estimate=cost,
        compiler_params=pltpu.CompilerParams(vmem_limit_bytes=vmem * 2**20),
    )(*args)


def begin(*triples):
    copies = [pltpu.make_async_copy(*triple) for triple in triples]
    for copy in copies:
        copy.start()
    return copies


def struct(shape, dtype):
    return jax.ShapeDtypeStruct(shape, dtype)


def route_kernel(count_ref, row_ref, owner_ref, bag_ref, table_ref, send_ref, at_ref):
    eye = subs((SLOTS, SLOTS)) == lanes((SLOTS, SLOTS))

    def column(ref):
        return jnp.sum(jnp.where(eye, ref[...].astype(F32), 0.0), axis=1, keepdims=True)

    row, bag = column(row_ref), column(bag_ref)
    owner = column(owner_ref)
    live = subs((SLOTS, BLOCK)) < count_ref[0]
    hits = jnp.where((owner == lanes((SLOTS, BLOCK)).astype(F32)) & live, 1.0, 0.0)
    before = one_hot(subs((SLOTS, SLOTS)) > lanes((SLOTS, SLOTS)))
    earlier = dot(before, hits.astype(BF16), NN)
    place = jnp.sum(earlier * hits, axis=1, keepdims=True)
    alive = jnp.sum(hits, axis=1, keepdims=True)
    target = jnp.where(alive > 0.5, owner * CAP + place, -1.0)
    at = one_hot(target == lanes((SLOTS, ROWS * CAP)).astype(F32))
    at_ref[...] = at
    looked = dot(one_hot(row == lanes((SLOTS, 1024)).astype(F32)), table_ref[...], NN)
    both = jnp.concatenate(
        [looked.astype(BF16), jnp.broadcast_to(bag, (SLOTS, BLOCK)).astype(BF16)], axis=1
    )
    sent = dot(at, both, TN)
    send_ref[...] = jnp.concatenate(
        [
            sent[:, :BLOCK].reshape(ROWS, CAP, BLOCK),
            sent[:, BLOCK:].reshape(ROWS, CAP, BLOCK),
        ],
        axis=1,
    ).astype(BF16)


def pool_kernel(got_ref, own_ref, meta_ref, out_ref):
    got = got_ref[...].astype(F32)
    data = got[:, :CAP].reshape(ROWS * CAP, BLOCK).astype(BF16)
    bags = got[:, CAP:].reshape(ROWS * CAP, BLOCK)
    hot = one_hot(bags == lanes((ROWS * CAP, BLOCK)).astype(F32))
    pooled = dot(hot, data, TN)[:BATCH].astype(BF16).astype(F32)
    eye = subs((BLOCK, BLOCK)) == lanes((BLOCK, BLOCK))
    bag_rows = [
        jnp.sum(jnp.where(eye, bags[i * BLOCK : (i + 1) * BLOCK], 0.0), axis=0, keepdims=True)
        for i in range(4)
    ]
    meta = meta_ref[...].astype(F32)
    meta = jnp.concatenate([meta[:4], *bag_rows, meta[8:]], axis=0).astype(BF16)
    own = own_ref[...].astype(F32)
    part = jnp.concatenate([pooled, own[:, : 3 * BLOCK]], axis=1)
    ids = own[:, 3 * BLOCK : 3 * BLOCK + SLICE]
    for c in range(COLS):
        top = jnp.concatenate([part[:, c * SLICE : (c + 1) * SLICE], ids], axis=1)
        out_ref[c, :BATCH, :] = top.astype(BF16)
        out_ref[c, BATCH:, :] = meta


def cross_kernel(
    got_ref,
    tables_far,
    left_far,
    right_far,
    weight_far,
    bias_far,
    out_ref,
    x_far,
    counts_far,
    left_end_ref,
    right_end_ref,
    ends_ref,
    tables_ref,
    left_ref,
    right_ref,
    weight_ref,
    bias_ref,
    x_ref,
    counts_ref,
    *sems,
):
    tables_in, weight_in, bias_in, left_in, right_in = begin(
        (tables_far, tables_ref, sems[0]),
        (weight_far, weight_ref, sems[1]),
        (bias_far, bias_ref, sems[2]),
        (left_far, left_ref, sems[3]),
        (right_far, right_ref, sems[4]),
    )
    ids = got_ref[:, :BATCH, SLICE:].astype(F32).reshape(HOST, SLICE)
    part = got_ref[:, :BATCH, :SLICE].astype(F32).reshape(HOST, SLICE)
    name = lanes((HOST, NAMES)).astype(F32)
    for t in range(TABLES):
        count = jnp.zeros((HOST, NAMES), F32)
        for j in range(4):
            count += jnp.where(ids[:, 4 * t + j : 4 * t + j + 1] == name, 1.0, 0.0)
        counts_ref[t] = count.astype(BF16)
    (counts_out,) = begin((counts_ref, counts_far, sems[5]))
    tables_in.wait()
    pieces = []
    for t in range(TABLES):
        pieces.append(dot(counts_ref[t], tables_ref[t], NT))
        if t % 2:
            x_ref[:, (t // 2) * BLOCK : (t // 2 + 1) * BLOCK] = jnp.concatenate(
                pieces, axis=1
            ).astype(BF16)
            pieces = []
    x_ref[:, WIDE - BLOCK :] = jnp.concatenate(pieces + [part], axis=1).astype(BF16)
    (x_out,) = begin((x_ref, x_far, sems[6]))
    for copy in (weight_in, bias_in, left_in, right_in):
        copy.wait()
    low_rank = jnp.zeros((HOST, RANK), F32)
    back = jnp.zeros((HOST, RANK), F32)
    plain = jnp.zeros((HOST, 1), F32)
    for n in range(4):
        cols = slice(n * 256, (n + 1) * 256)
        x = x_ref[:, cols]
        weighted = x.astype(F32) * weight_ref[:, cols]
        low_rank += dot(x, left_ref[cols, :], NN)
        back += dot(weighted.astype(BF16), right_ref[:, cols], NT)
        plain += jnp.sum(weighted * (bias_ref[:, cols] + 1.0), axis=1, keepdims=True)
    high = plain.astype(BF16).astype(F32)
    lane = lanes((HOST, BLOCK))
    rest = jnp.where(lane == 0, high, jnp.where(lane == 1, plain - high, 0.0))
    out_ref[:, :, :RANK] = low_rank.astype(BF16).reshape(COLS, BATCH, RANK)
    out_ref[:, :, RANK : 2 * RANK] = back.astype(BF16).reshape(COLS, BATCH, RANK)
    out_ref[:, :, 2 * RANK :] = rest.astype(BF16).reshape(COLS, BATCH, BLOCK)
    left_end_ref[...] = left_ref[WIDE - BLOCK :, :]
    right_end_ref[...] = right_ref[:, WIDE - BLOCK :]
    ends_ref[0:1, :] = weight_ref[:, WIDE - BLOCK :]
    ends_ref[1:2, :] = bias_ref[:, WIDE - BLOCK :]
    for copy in (counts_out, x_out):
        copy.wait()


def residue_kernel(got_ref, label_ref, out_ref):
    total = got_ref[0].astype(F32)
    for c in range(1, COLS):
        total += got_ref[c].astype(F32)
    low_rank = total[:, :RANK].astype(BF16).astype(F32)
    back = total[:, RANK : 2 * RANK]
    plain = total[:, 2 * RANK : 2 * RANK + 1] + total[:, 2 * RANK + 1 : 2 * RANK + 2]
    logits = jnp.sum(low_rank * back, axis=1, keepdims=True) + plain
    eye = subs((BATCH, BATCH)) == lanes((BATCH, BATCH))
    label = jnp.sum(jnp.where(eye, label_ref[...].astype(F32), 0.0), axis=1, keepdims=True)
    residue = (jax.nn.sigmoid(logits) - label) * LOSS_SCALE
    high = residue.astype(BF16).astype(F32)
    lane = lanes((BATCH, BLOCK))
    rest = jnp.where(lane == 0, high, jnp.where(lane == 1, residue - high, 0.0))
    block = jnp.concatenate([low_rank, residue * back, rest], axis=1).astype(BF16)
    for c in range(COLS):
        out_ref[c] = block


def part_kernel(got_ref, left_ref, right_ref, ends_ref, out_far, out_ref, out_sem):
    low_rank = got_ref[:, :, :RANK].reshape(HOST, RANK)
    grad_rank = got_ref[:, :, RANK : 2 * RANK].reshape(HOST, RANK)
    rest = got_ref[:, :, 2 * RANK :].astype(F32).reshape(HOST, BLOCK)
    residue = rest[:, 0:1] + rest[:, 1:2]
    expanded = dot(low_rank, right_ref[...], NN) + ends_ref[1:2, :]
    grad = residue * ends_ref[0:1, :] * (expanded + 1.0) + dot(grad_rank, left_ref[...], NT)
    out_ref[...] = grad.astype(BF16).reshape(COLS, BATCH, BLOCK)
    (copy,) = begin((out_ref, out_far, out_sem))
    copy.wait()


def order(odd, r):
    z, y = r // SIDE, r % SIDE
    return jnp.where(odd == 1, z, y), jnp.where(odd == 1, y, z)


def grads_kernel(
    got_ref,
    x_far,
    counts_far,
    left_far,
    right_far,
    weight_far,
    bias_far,
    out_ref,
    x_ref,
    counts_ref,
    left_ref,
    right_ref,
    weight_ref,
    bias_ref,
    band_ref,
    grad_ref,
    vector_ref,
    *sems,
):
    right_in, x_in, weight_in, bias_in, left_in, counts_in = begin(
        (right_far, right_ref, sems[0]),
        (x_far, x_ref, sems[1]),
        (weight_far, weight_ref, sems[2]),
        (bias_far, bias_ref, sems[3]),
        (left_far, left_ref, sems[4]),
        (counts_far, counts_ref, sems[5]),
    )
    odd = lax.axis_index("col") % 2
    for copy in (right_in, x_in, weight_in, bias_in):
        copy.wait()
    low_rank = got_ref[:, :, :RANK].reshape(HOST, RANK)
    grad_rank = got_ref[:, :, RANK : 2 * RANK].reshape(HOST, RANK)
    rest = got_ref[:, :, 2 * RANK :].astype(F32).reshape(HOST, BLOCK)
    residue = rest[:, 0:1] + rest[:, 1:2]
    for n in range(4):
        cols = slice(n * 256, (n + 1) * 256)
        x = x_ref[:, cols]
        wide = x.astype(F32)
        expanded = dot(low_rank, right_ref[:, cols], NN) + bias_ref[:, cols]
        vector_ref[1:2, cols] = jnp.sum(
            residue * (wide * expanded + wide), axis=0, keepdims=True
        )
        grad_crossed = residue * weight_ref[:, cols]
        grad_expanded = grad_crossed * wide
        vector_ref[0:1, cols] = jnp.sum(grad_expanded, axis=0, keepdims=True)
        grad_ref[:, cols] = grad_crossed * (expanded + 1.0)
        band_ref[:, cols] = dot(low_rank, grad_expanded.astype(BF16), TN)
        left = dot(x, grad_rank, TN).astype(BF16)
        for i in range(16):
            a, b = order(odd, 16 * n + i)
            out_ref[a, b, :, :RANK] = left[16 * i : 16 * i + 16]
    for r in range(ROWS):
        a, b = order(odd, r)
        band = band_ref[8 * r : 8 * r + 8, :]
        out_ref[a, b, :, RANK : 2 * RANK] = jnp.concatenate(
            [band[:, :RANK], band[:, RANK:]], axis=0
        ).astype(BF16)
    blank = jnp.zeros((12, SLICE), F32)
    vectors = []
    for b in range(SIDE):
        pieces = [
            vector_ref[v : v + 1, b * BLOCK + h * SLICE : b * BLOCK + (h + 1) * SLICE]
            for v in range(2)
            for h in range(2)
        ]
        vector = jnp.concatenate(pieces + [blank], axis=0)
        vectors.append(jnp.concatenate([vector, jnp.zeros((16, SLICE), F32)], axis=1))
    out_ref[:, :, :, SUMS:] = jnp.broadcast_to(
        jnp.stack(vectors, axis=0)[None], (SIDE, SIDE, 16, BLOCK)
    ).astype(BF16)
    left_in.wait()
    counts_in.wait()
    for n in range(4):
        cols = slice(n * 256, (n + 1) * 256)
        grad = grad_ref[:, cols] + dot(grad_rank, left_ref[cols, :], NT)
        grad = grad.astype(BF16).T
        for i in range(4):
            t = 4 * n + i
            if t < TABLES:
                medium = dot(grad[i * SLICE : (i + 1) * SLICE], counts_ref[t], NN).astype(BF16)
            else:
                medium = jnp.zeros((SLICE, NAMES), BF16)
            for k in range(4):
                a, b = order(odd, 4 * t + k)
                out_ref[a, b, :, 2 * RANK : SUMS] = medium[16 * k : 16 * k + 16]

def back_kernel(
    part_far, meta_far, sent_far, out_far, sample_far, part_ref, meta_ref, out_ref, sample_ref, *sems
):
    del sent_far
    col = lax.axis_index("col")
    last = out_far.at[:, :, :, SUMS:]
    copies = begin(
        (part_far, part_ref, sems[0]),
        (meta_far.at[col, BATCH : BATCH + 16], meta_ref, sems[1]),
        (last, out_ref, sems[2]),
    )
    odd = col % 2
    for copy in copies:
        copy.wait()
    grads = jnp.concatenate(
        [part_ref[c].astype(F32)[:, SLICE:] for c in range(COLS)], axis=1
    )
    sample_ref[...] = grads.astype(BF16)
    sent = begin((sample_ref, sample_far, sems[3]))
    meta = meta_ref[...].astype(F32)
    bags = jnp.concatenate([meta[4 + i : 5 + i] for i in range(4)], axis=1)
    hot = one_hot(bags == subs((BATCH, ROWS * CAP)).astype(F32))
    back = dot(hot, grads[:, :BLOCK].astype(BF16), TN).reshape(ROWS, CAP, BLOCK)
    back = jnp.concatenate([back[:, :, :SLICE], back[:, :, SLICE:]], axis=1)
    back = jnp.concatenate([back, back], axis=2)
    first = lanes((16, BLOCK)) < SLICE
    for r in range(ROWS):
        a, b = order(odd, r)
        out_ref[a, b] = jnp.where(first, out_ref[a, b].astype(F32), back[r]).astype(BF16)
    sent += begin((out_ref, last, sems[4]))
    for copy in sent:
        copy.wait()


SUMS = 2 * RANK + NAMES


def middle_kernel(got_ref, out_ref):
    vectors = []
    for b in range(SIDE):
        total = got_ref[0, b].astype(F32)
        for a in range(1, SIDE):
            total += got_ref[a, b].astype(F32)
        out_ref[b, :, :SUMS] = total[:, :SUMS].astype(BF16)
        vectors.append(total[:4, SUMS : SUMS + SLICE])
        for a in range(0, SIDE, 2):
            pair = [got_ref[a + i, b, :, SUMS + SLICE :].astype(F32) for i in range(2)]
            at = SUMS + a * SLICE
            out_ref[b, :, at : at + BLOCK] = jnp.concatenate(pair, axis=1).astype(BF16)
    packed = jnp.concatenate(
        [jnp.concatenate(vectors[:4], axis=0), jnp.concatenate(vectors[4:], axis=0)], axis=1
    ).astype(BF16)
    for b in range(SIDE):
        out_ref[b, :, SUMS + 512 :] = packed


def last_kernel(got_ref, left_ref, right_ref, bias_ref, top_ref, medium_ref):
    sums = got_ref[0, :, :SUMS].astype(F32)
    packed = got_ref[0, :, SUMS + 512 :].astype(F32)
    for a in range(1, SIDE):
        sums += got_ref[a, :, :SUMS].astype(F32)
        packed += got_ref[a, :, SUMS + 512 :].astype(F32)
    medium = sums[:, 2 * RANK :].astype(BF16)
    for r in range(ROWS):
        medium_ref[r] = medium
    left_ref[...] = sums[:, :RANK]
    right = sums[:, RANK : 2 * RANK]
    right_ref[...] = jnp.concatenate([right[:8], right[8:]], axis=1)
    for v, ref in ((0, bias_ref), (2, top_ref)):
        pieces = []
        for b in range(SIDE):
            at = (b // 4) * SLICE
            for h in range(2):
                i = 4 * (b % 4) + v + h
                pieces.append(packed[i : i + 1, at : at + SLICE])
        ref[...] = jnp.concatenate(pieces, axis=1)


def slots_kernel(got_ref, at_ref, out_ref, data_scr):
    odd = lax.axis_index("col") % 2
    for second in range(SIDE):
        for first in range(SIDE):
            at = SUMS + first * SLICE
            block = got_ref[second, :, at : at + SLICE].astype(F32)
            r = jnp.where(odd == 1, first * SIDE + second, second * SIDE + first)
            data_scr[r] = jnp.concatenate([block[:CAP], block[CAP:]], axis=1)
    data = data_scr[...].reshape(ROWS * CAP, BLOCK).astype(BF16)
    out_ref[0] = dot(at_ref[...], data, NN).astype(BF16)


def tables_kernel(
    got_ref, meta_ref, medium_ref, out_far, medium_far, out_ref, wide_ref, out_sem, wide_sem
):
    for t in range(TABLES):
        wide_ref[t] = medium_ref[4 * t : 4 * t + 4].astype(F32).reshape(SLICE, NAMES)
    copies = begin((wide_ref, medium_far, wide_sem))
    row = subs((1024, SLOTS)).astype(F32)
    total = jnp.zeros((1024, BLOCK), F32)
    for c in range(COLS):
        meta = meta_ref[c, BATCH : BATCH + 16, :].astype(F32)
        name = jnp.concatenate(
            [meta[i : i + 1] * 32.0 + meta[2 + i : 3 + i] for i in range(2)], axis=1
        )
        total += dot(one_hot(name == row), got_ref[c], NN)
    out_ref[...] = total
    copies += begin((out_ref, out_far, out_sem))
    for copy in copies:
        copy.wait()


def sides():
    first, second = [], []
    for c in range(COLS):
        for k in range(SIDE):
            along_y = [(k * SIDE + y) * COLS + c for y in range(SIDE)]
            along_z = [(z * SIDE + k) * COLS + c for z in range(SIDE)]
            first.append(along_z if c % 2 else along_y)
            second.append(along_y if c % 2 else along_z)
    return first, second


def swap(value, axis, groups=None):
    return lax.all_to_all(
        value, axis, split_axis=0, concat_axis=0, tiled=True, axis_index_groups=groups
    )


def body(
    giant_table,
    look_row,
    look_owner,
    look_bag,
    look_count,
    medium_tables,
    medium_ids,
    medium_lengths,
    dense_features,
    click_labels,
    cross_left,
    cross_right,
    cross_bias,
    top_weight,
):
    first, second = sides()
    bias, weight = cross_bias.reshape(1, WIDE), top_weight.reshape(1, WIDE)
    live = jnp.arange(4)[None, None, :] < medium_lengths[:, :, None]
    ids = jnp.where(live, medium_ids, NAMES).reshape(BATCH, 4 * TABLES).astype(BF16)
    ids = jnp.pad(ids, ((0, 0), (0, BLOCK - 4 * TABLES)))
    own = jnp.concatenate([dense_features, ids], axis=1)
    names = jnp.concatenate([look_row // 32, look_row % 32]).astype(BF16).reshape(4, BLOCK)
    names = jnp.pad(names, ((0, 12), (0, 0)))

    look_row = look_row.reshape(1, SLOTS)
    send, at = call(
        route_kernel,
        (struct((ROWS, 2 * CAP, BLOCK), BF16), struct((SLOTS, ROWS * CAP), BF16)),
        look_count,
        look_row,
        look_owner.reshape(1, SLOTS),
        look_bag.reshape(1, SLOTS),
        giant_table,
        smem=(0,),
        vmem=60,
    )
    got = swap(send, "row")
    send = call(
        pool_kernel,
        struct((COLS, 48, BLOCK), BF16),
        got,
        own,
        names,
    )
    meta = swap(send, "col")
    send, x, counts, left_end, right_end, ends = call(
        cross_kernel,
        (
            pltpu.VMEM((COLS, BATCH, 2 * RANK + BLOCK), BF16),
            pltpu.HBM((HOST, WIDE), BF16),
            pltpu.HBM((TABLES, HOST, NAMES), BF16),
            struct((BLOCK, RANK), BF16),
            struct((RANK, BLOCK), BF16),
            struct((2, BLOCK), F32),
        ),
        meta,
        jnp.swapaxes(medium_tables, 1, 2),
        cross_left,
        cross_right,
        weight,
        bias,
        far=(1, 2, 3, 4, 5),
        pinned=(1, 2, 3, 4, 5),
        far_outs=(1, 2),
        scratch=(
            pltpu.VMEM((TABLES, SLICE, NAMES), BF16),
            pltpu.VMEM((WIDE, RANK), BF16),
            pltpu.VMEM((RANK, WIDE), BF16),
            pltpu.VMEM((1, WIDE), F32),
            pltpu.VMEM((1, WIDE), F32),
            pltpu.VMEM((HOST, WIDE), BF16),
            pltpu.VMEM((TABLES, HOST, NAMES), BF16),
        ),
        copies=7,
        vmem=32,
    )
    got = swap(send, "col")
    send = call(
        residue_kernel,
        struct((COLS, BATCH, 2 * RANK + BLOCK), BF16),
        got,
        click_labels.reshape(1, BATCH),
    )
    ranks = swap(send, "col")
    send = call(
        part_kernel,
        struct((COLS, BATCH, BLOCK), BF16),
        ranks,
        left_end,
        right_end,
        ends,
        far_outs=(0,),
        scratch=(pltpu.VMEM((COLS, BATCH, BLOCK), BF16),),
        copies=1,
    )
    parts = swap(send, "col")
    send = call(
        grads_kernel,
        pltpu.VMEM((SIDE, SIDE, 16, SUMS + BLOCK), BF16),
        ranks,
        x,
        counts,
        cross_left,
        cross_right,
        weight,
        bias,
        far=range(1, 7),
        pinned=range(1, 7),
        scratch=(
            pltpu.VMEM((HOST, WIDE), BF16),
            pltpu.VMEM((TABLES, HOST, NAMES), BF16),
            pltpu.VMEM((WIDE, RANK), BF16),
            pltpu.VMEM((RANK, WIDE), BF16),
            pltpu.VMEM((1, WIDE), F32),
            pltpu.VMEM((1, WIDE), F32),
            pltpu.VMEM((RANK, WIDE), F32),
            pltpu.VMEM((HOST, WIDE), F32),
            pltpu.VMEM((2, WIDE), F32),
        ),
        copies=6,
        vmem=40,
        cost=pl.CostEstimate(flops=3 * 10**9, bytes_accessed=10**7, transcendentals=0),
    )
    send, sample_grads = call(
        back_kernel,
        (
            pltpu.VMEM((SIDE, SIDE, 16, SUMS + BLOCK), BF16),
            struct((BATCH, COLS * SLICE), BF16),
        ),
        parts,
        meta,
        send,
        free=(0, 1, 2),
        far_outs=(1,),
        free_outs=(0,),
        scratch=(
            pltpu.VMEM((COLS, BATCH, BLOCK), BF16),
            pltpu.VMEM((16, BLOCK), BF16),
            pltpu.VMEM((SIDE, SIDE, 16, BLOCK), BF16),
            pltpu.VMEM((BATCH, COLS * SLICE), BF16),
        ),
        copies=5,
        alias={2: 0},
        vmem=40,
    )
    got = swap(send, ("row", "col"), first)
    send = call(middle_kernel, struct((SIDE, 16, SUMS + 512 + BLOCK), BF16), got)
    got = swap(send, ("row", "col"), second)
    left_grad, right_grad, bias_grad, top_grad, medium = call(
        last_kernel,
        (
            struct((16, RANK), F32),
            struct((8, WIDE), F32),
            struct((1, WIDE), F32),
            struct((1, WIDE), F32),
            struct((ROWS, 16, NAMES), BF16),
        ),
        got,
    )
    medium = swap(medium, "row")
    slots = call(
        slots_kernel,
        struct((1, SLOTS, BLOCK), BF16),
        got,
        at,
        scratch=(pltpu.VMEM((ROWS, CAP, BLOCK), F32),),
    )
    giant_grad, medium_grad = call(
        tables_kernel,
        (struct((1024, BLOCK), F32), struct((TABLES, SLICE, NAMES), F32)),
        lax.all_gather(slots, "col", axis=0, tiled=True),
        meta,
        medium,
        far_outs=(0, 1),
        scratch=(pltpu.VMEM((1024, BLOCK), F32), pltpu.VMEM((TABLES, SLICE, NAMES), F32)),
        copies=2,
    )
    medium_grad = jnp.swapaxes(medium_grad, 1, 2)
    return (
        sample_grads,
        giant_grad,
        medium_grad,
        left_grad,
        right_grad,
        bias_grad.reshape(WIDE),
        top_grad.reshape(WIDE),
    )


def solution(mesh):
    both = P(("row", "col"))
    placed = (
        P("row", None),
        both,
        P(("row", "col"), None),
        both,
        both,
        P(None, None, "col"),
        P(("row", "col"), None, None),
        P(("row", "col"), None),
        P(("row", "col"), None),
        both,
        P("col", None),
        P(None, "col"),
        P("col"),
        P("col"),
    )
    return jax.shard_map(
        body,
        mesh=mesh,
        in_specs=placed,
        out_specs=(
            P(("row", "col"), None),
            P("row", None),
            P(None, None, "col"),
            P(("col", "row"), None),
            P("row", "col"),
            P("col"),
            P("col"),
        ),
        check_vma=False,
    )
```

```python
import functools

import jax
import jax.numpy as jnp
from jax import lax
from jax.experimental import pallas as pl
from jax.experimental.pallas import tpu as pltpu
from jax.sharding import PartitionSpec as P

LOSS_SCALE = 0.015625

F32, BF16, I32 = jnp.float32, jnp.bfloat16, jnp.int32
ROWS, COLS = 64, 8
SIDE = 8
BATCH, HOST = 32, 256
SLOTS, CAP = 256, 8
WIDE, RANK = 1024, 512
TABLES, NAMES, SLICE = 15, 256, 64
BLOCK = 128

NN = ((1,), (0,))
NT = ((1,), (1,))
TN = ((0,), (0,))


def dot(left, right, dims):
    return lax.dot_general(left, right, (dims, ((), ())), preferred_element_type=F32)


def lanes(shape):
    return lax.broadcasted_iota(I32, shape, len(shape) - 1)


def subs(shape):
    return lax.broadcasted_iota(I32, shape, len(shape) - 2)


def one_hot(mask):
    return jnp.where(mask, 1.0, 0.0).astype(BF16)


def call(
    kernel,
    outs,
    *args,
    smem=(),
    far=(),
    far_outs=(),
    scratch=(),
    copies=0,
    vmem=16,
    alias=None,
    cost=None,
    pinned=(),
    free=(),
    free_outs=(),
):
    single = not isinstance(outs, tuple)
    args = [
        pltpu.with_memory_space_constraint(arg, pltpu.HBM) if i in pinned else arg
        for i, arg in enumerate(args)
    ]
    specs = tuple(
        pl.BlockSpec(
            memory_space=pl.ANY
            if i in free_outs
            else pltpu.HBM
            if i in far_outs
            else pltpu.VMEM
        )
        for i in range(1 if single else len(outs))
    )
    return pl.pallas_call(
        kernel,
        out_shape=outs,
        in_specs=[
            pl.BlockSpec(
                memory_space=pltpu.SMEM
                if i in smem
                else pl.ANY
                if i in free
                else pltpu.HBM
                if i in far
                else pltpu.VMEM
            )
            for i in range(len(args))
        ],
        out_specs=specs[0] if single else specs,
        scratch_shapes=[*scratch, *[pltpu.SemaphoreType.DMA] * copies],
        input_output_aliases=alias or {},
        cost_estimate=cost,
        compiler_params=pltpu.CompilerParams(vmem_limit_bytes=vmem * 2**20),
    )(*args)


def begin(*triples):
    copies = [pltpu.make_async_copy(*triple) for triple in triples]
    for copy in copies:
        copy.start()
    return copies


def struct(shape, dtype):
    return jax.ShapeDtypeStruct(shape, dtype)


def route_kernel(count_ref, row_ref, owner_ref, bag_ref, table_ref, send_ref, at_ref):
    eye = subs((SLOTS, SLOTS)) == lanes((SLOTS, SLOTS))

    def column(ref):
        return jnp.sum(jnp.where(eye, ref[...].astype(F32), 0.0), axis=1, keepdims=True)

    row, bag = column(row_ref), column(bag_ref)
    owner = column(owner_ref)
    live = subs((SLOTS, BLOCK)) < count_ref[0]
    hits = jnp.where((owner == lanes((SLOTS, BLOCK)).astype(F32)) & live, 1.0, 0.0)
    before = one_hot(subs((SLOTS, SLOTS)) > lanes((SLOTS, SLOTS)))
    earlier = dot(before, hits.astype(BF16), NN)
    place = jnp.sum(earlier * hits, axis=1, keepdims=True)
    alive = jnp.sum(hits, axis=1, keepdims=True)
    target = jnp.where(alive > 0.5, owner * CAP + place, -1.0)
    at = one_hot(target == lanes((SLOTS, ROWS * CAP)).astype(F32))
    at_ref[...] = at
    looked = dot(one_hot(row == lanes((SLOTS, 1024)).astype(F32)), table_ref[...], NN)
    both = jnp.concatenate(
        [looked.astype(BF16), jnp.broadcast_to(bag, (SLOTS, BLOCK)).astype(BF16)], axis=1
    )
    sent = dot(at, both, TN)
    send_ref[...] = jnp.concatenate(
        [
            sent[:, :BLOCK].reshape(ROWS, CAP, BLOCK),
            sent[:, BLOCK:].reshape(ROWS, CAP, BLOCK),
        ],
        axis=1,
    ).astype(BF16)


def pool_kernel(got_ref, own_ref, meta_ref, out_ref):
    got = got_ref[...].astype(F32)
    data = got[:, :CAP].reshape(ROWS * CAP, BLOCK).astype(BF16)
    bags = got[:, CAP:].reshape(ROWS * CAP, BLOCK)
    hot = one_hot(bags == lanes((ROWS * CAP, BLOCK)).astype(F32))
    pooled = dot(hot, data, TN)[:BATCH].astype(BF16).astype(F32)
    eye = subs((BLOCK, BLOCK)) == lanes((BLOCK, BLOCK))
    bag_rows = [
        jnp.sum(jnp.where(eye, bags[i * BLOCK : (i + 1) * BLOCK], 0.0), axis=0, keepdims=True)
        for i in range(4)
    ]
    meta = meta_ref[...].astype(F32)
    meta = jnp.concatenate([meta[:4], *bag_rows, meta[8:]], axis=0).astype(BF16)
    own = own_ref[...].astype(F32)
    part = jnp.concatenate([pooled, own[:, : 3 * BLOCK]], axis=1)
    ids = own[:, 3 * BLOCK : 3 * BLOCK + SLICE]
    for c in range(COLS):
        top = jnp.concatenate([part[:, c * SLICE : (c + 1) * SLICE], ids], axis=1)
        out_ref[c, :BATCH, :] = top.astype(BF16)
        out_ref[c, BATCH:, :] = meta


def cross_kernel(
    got_ref,
    tables_far,
    left_far,
    right_far,
    weight_far,
    bias_far,
    out_ref,
    x_far,
    counts_far,
    left_end_ref,
    right_end_ref,
    ends_ref,
    own_ref,
    tables_ref,
    left_ref,
    right_ref,
    weight_ref,
    bias_ref,
    x_ref,
    counts_ref,
    *sems,
):
    tables_in, weight_in, bias_in, left_in, right_in = begin(
        (tables_far, tables_ref, sems[0]),
        (weight_far, weight_ref, sems[1]),
        (bias_far, bias_ref, sems[2]),
        (left_far, left_ref, sems[3]),
        (right_far, right_ref, sems[4]),
    )
    ids = got_ref[:, :BATCH, SLICE:].astype(F32).reshape(HOST, SLICE)
    part = got_ref[:, :BATCH, :SLICE].astype(F32).reshape(HOST, SLICE)
    name = lanes((HOST, NAMES)).astype(F32)
    for t in range(TABLES):
        count = jnp.zeros((HOST, NAMES), F32)
        for j in range(4):
            count += jnp.where(ids[:, 4 * t + j : 4 * t + j + 1] == name, 1.0, 0.0)
        counts_ref[t] = count.astype(BF16)
    (counts_out,) = begin((counts_ref, counts_far, sems[5]))
    tables_in.wait()
    pieces = []
    for t in range(TABLES):
        pieces.append(dot(counts_ref[t], tables_ref[t], NT))
        if t % 2:
            x_ref[:, (t // 2) * BLOCK : (t // 2 + 1) * BLOCK] = jnp.concatenate(
                pieces, axis=1
            ).astype(BF16)
            pieces = []
    x_ref[:, WIDE - BLOCK :] = jnp.concatenate(pieces + [part], axis=1).astype(BF16)
    (x_out,) = begin((x_ref, x_far, sems[6]))
    for copy in (weight_in, bias_in, left_in, right_in):
        copy.wait()
    low_rank = jnp.zeros((HOST, RANK), F32)
    back = jnp.zeros((HOST, RANK), F32)
    plain = jnp.zeros((HOST, 1), F32)
    for n in range(4):
        cols = slice(n * 256, (n + 1) * 256)
        x = x_ref[:, cols]
        weighted = x.astype(F32) * weight_ref[:, cols]
        low_rank += dot(x, left_ref[cols, :], NN)
        back += dot(weighted.astype(BF16), right_ref[:, cols], NT)
        plain += jnp.sum(weighted * (bias_ref[:, cols] + 1.0), axis=1, keepdims=True)
    high = plain.astype(BF16).astype(F32)
    lane = lanes((HOST, BLOCK))
    rest = jnp.where(lane == 0, high, jnp.where(lane == 1, plain - high, 0.0))
    out_ref[:, :, :RANK] = low_rank.astype(BF16).reshape(COLS, BATCH, RANK)
    out_ref[:, :, RANK : 2 * RANK] = back.astype(BF16).reshape(COLS, BATCH, RANK)
    out_ref[:, :, 2 * RANK :] = rest.astype(BF16).reshape(COLS, BATCH, BLOCK)
    own_ref[...] = got_ref[lax.axis_index("col"), BATCH : BATCH + 16, :]
    left_end_ref[...] = left_ref[WIDE - BLOCK :, :]
    right_end_ref[...] = right_ref[:, WIDE - BLOCK :]
    ends_ref[0:1, :] = weight_ref[:, WIDE - BLOCK :]
    ends_ref[1:2, :] = bias_ref[:, WIDE - BLOCK :]
    for copy in (counts_out, x_out):
        copy.wait()


def residue_kernel(got_ref, label_ref, out_ref):
    total = got_ref[0].astype(F32)
    for c in range(1, COLS):
        total += got_ref[c].astype(F32)
    low_rank = total[:, :RANK].astype(BF16).astype(F32)
    back = total[:, RANK : 2 * RANK]
    plain = total[:, 2 * RANK : 2 * RANK + 1] + total[:, 2 * RANK + 1 : 2 * RANK + 2]
    logits = jnp.sum(low_rank * back, axis=1, keepdims=True) + plain
    eye = subs((BATCH, BATCH)) == lanes((BATCH, BATCH))
    label = jnp.sum(jnp.where(eye, label_ref[...].astype(F32), 0.0), axis=1, keepdims=True)
    residue = (jax.nn.sigmoid(logits) - label) * LOSS_SCALE
    high = residue.astype(BF16).astype(F32)
    lane = lanes((BATCH, BLOCK))
    rest = jnp.where(lane == 0, high, jnp.where(lane == 1, residue - high, 0.0))
    block = jnp.concatenate([low_rank, residue * back, rest], axis=1).astype(BF16)
    for c in range(COLS):
        out_ref[c] = block


def part_kernel(got_ref, left_ref, right_ref, ends_ref, out_far, out_ref, out_sem):
    low_rank = got_ref[:, :, :RANK].reshape(HOST, RANK)
    grad_rank = got_ref[:, :, RANK : 2 * RANK].reshape(HOST, RANK)
    rest = got_ref[:, :, 2 * RANK :].astype(F32).reshape(HOST, BLOCK)
    residue = rest[:, 0:1] + rest[:, 1:2]
    expanded = dot(low_rank, right_ref[...], NN) + ends_ref[1:2, :]
    grad = residue * ends_ref[0:1, :] * (expanded + 1.0) + dot(grad_rank, left_ref[...], NT)
    out_ref[...] = grad.astype(BF16).reshape(COLS, BATCH, BLOCK)
    (copy,) = begin((out_ref, out_far, out_sem))
    copy.wait()


def order(odd, r):
    z, y = r // SIDE, r % SIDE
    return jnp.where(odd == 1, z, y), jnp.where(odd == 1, y, z)


def grads_kernel(
    got_ref,
    x_far,
    counts_far,
    left_far,
    right_far,
    weight_far,
    bias_far,
    out_ref,
    x_ref,
    counts_ref,
    left_ref,
    right_ref,
    weight_ref,
    bias_ref,
    band_ref,
    grad_ref,
    vector_ref,
    *sems,
):
    right_in, x_in, weight_in, bias_in, left_in, counts_in = begin(
        (right_far, right_ref, sems[0]),
        (x_far, x_ref, sems[1]),
        (weight_far, weight_ref, sems[2]),
        (bias_far, bias_ref, sems[3]),
        (left_far, left_ref, sems[4]),
        (counts_far, counts_ref, sems[5]),
    )
    odd = lax.axis_index("col") % 2
    for copy in (right_in, x_in, weight_in, bias_in):
        copy.wait()
    low_rank = got_ref[:, :, :RANK].reshape(HOST, RANK)
    grad_rank = got_ref[:, :, RANK : 2 * RANK].reshape(HOST, RANK)
    rest = got_ref[:, :, 2 * RANK :].astype(F32).reshape(HOST, BLOCK)
    residue = rest[:, 0:1] + rest[:, 1:2]
    for n in range(4):
        cols = slice(n * 256, (n + 1) * 256)
        x = x_ref[:, cols]
        wide = x.astype(F32)
        expanded = dot(low_rank, right_ref[:, cols], NN) + bias_ref[:, cols]
        vector_ref[1:2, cols] = jnp.sum(
            residue * (wide * expanded + wide), axis=0, keepdims=True
        )
        grad_crossed = residue * weight_ref[:, cols]
        grad_expanded = grad_crossed * wide
        vector_ref[0:1, cols] = jnp.sum(grad_expanded, axis=0, keepdims=True)
        grad_ref[:, cols] = grad_crossed * (expanded + 1.0)
        band_ref[:, cols] = dot(low_rank, grad_expanded.astype(BF16), TN)
        left = dot(x, grad_rank, TN).astype(BF16)
        for i in range(16):
            a, b = order(odd, 16 * n + i)
            out_ref[a, b, :, :RANK] = left[16 * i : 16 * i + 16]
    for r in range(ROWS):
        a, b = order(odd, r)
        band = band_ref[8 * r : 8 * r + 8, :]
        out_ref[a, b, :, RANK : 2 * RANK] = jnp.concatenate(
            [band[:, :RANK], band[:, RANK:]], axis=0
        ).astype(BF16)
    blank = jnp.zeros((12, SLICE), F32)
    vectors = []
    for b in range(SIDE):
        pieces = [
            vector_ref[v : v + 1, b * BLOCK + h * SLICE : b * BLOCK + (h + 1) * SLICE]
            for v in range(2)
            for h in range(2)
        ]
        vector = jnp.concatenate(pieces + [blank], axis=0)
        vectors.append(jnp.concatenate([vector, jnp.zeros((16, SLICE), F32)], axis=1))
    out_ref[:, :, :, SUMS:] = jnp.broadcast_to(
        jnp.stack(vectors, axis=0)[None], (SIDE, SIDE, 16, BLOCK)
    ).astype(BF16)
    left_in.wait()
    counts_in.wait()
    for n in range(4):
        cols = slice(n * 256, (n + 1) * 256)
        grad = grad_ref[:, cols] + dot(grad_rank, left_ref[cols, :], NT)
        grad = grad.astype(BF16).T
        for i in range(4):
            t = 4 * n + i
            if t < TABLES:
                medium = dot(grad[i * SLICE : (i + 1) * SLICE], counts_ref[t], NN).astype(BF16)
            else:
                medium = jnp.zeros((SLICE, NAMES), BF16)
            for k in range(4):
                a, b = order(odd, 4 * t + k)
                out_ref[a, b, :, 2 * RANK : SUMS] = medium[16 * k : 16 * k + 16]

def back_kernel(
    part_far, meta_ref, sent_far, out_far, sample_far, part_ref, out_ref, sample_ref, *sems
):
    del sent_far
    col = lax.axis_index("col")
    last = out_far.at[:, :, :, SUMS:]
    copies = begin(
        (part_far, part_ref, sems[0]),
        (last, out_ref, sems[1]),
    )
    odd = col % 2
    for copy in copies:
        copy.wait()
    grads = jnp.concatenate(
        [part_ref[c].astype(F32)[:, SLICE:] for c in range(COLS)], axis=1
    )
    sample_ref[...] = grads.astype(BF16)
    sent = begin((sample_ref, sample_far, sems[2]))
    meta = meta_ref[...].astype(F32)
    bags = jnp.concatenate([meta[4 + i : 5 + i] for i in range(4)], axis=1)
    hot = one_hot(bags == subs((BATCH, ROWS * CAP)).astype(F32))
    back = dot(hot, grads[:, :BLOCK].astype(BF16), TN).reshape(ROWS, CAP, BLOCK)
    back = jnp.concatenate([back[:, :, :SLICE], back[:, :, SLICE:]], axis=1)
    back = jnp.concatenate([back, back], axis=2)
    first = lanes((16, BLOCK)) < SLICE
    for r in range(ROWS):
        a, b = order(odd, r)
        out_ref[a, b] = jnp.where(first, out_ref[a, b].astype(F32), back[r]).astype(BF16)
    sent += begin((out_ref, last, sems[3]))
    for copy in sent:
        copy.wait()


SUMS = 2 * RANK + NAMES


def middle_kernel(got_ref, out_ref):
    vectors = []
    for b in range(SIDE):
        total = got_ref[0, b].astype(F32)
        for a in range(1, SIDE):
            total += got_ref[a, b].astype(F32)
        out_ref[b, :, :SUMS] = total[:, :SUMS].astype(BF16)
        vectors.append(total[:4, SUMS : SUMS + SLICE])
        for a in range(0, SIDE, 2):
            pair = [got_ref[a + i, b, :, SUMS + SLICE :].astype(F32) for i in range(2)]
            at = SUMS + a * SLICE
            out_ref[b, :, at : at + BLOCK] = jnp.concatenate(pair, axis=1).astype(BF16)
    packed = jnp.concatenate(
        [jnp.concatenate(vectors[:4], axis=0), jnp.concatenate(vectors[4:], axis=0)], axis=1
    ).astype(BF16)
    for b in range(SIDE):
        out_ref[b, :, SUMS + 512 :] = packed


def last_kernel(got_ref, left_ref, right_ref, bias_ref, top_ref, medium_ref):
    sums = got_ref[0, :, :SUMS].astype(F32)
    packed = got_ref[0, :, SUMS + 512 :].astype(F32)
    for a in range(1, SIDE):
        sums += got_ref[a, :, :SUMS].astype(F32)
        packed += got_ref[a, :, SUMS + 512 :].astype(F32)
    medium = sums[:, 2 * RANK :].astype(BF16)
    for r in range(ROWS):
        medium_ref[r] = medium
    left_ref[...] = sums[:, :RANK]
    right = sums[:, RANK : 2 * RANK]
    right_ref[...] = jnp.concatenate([right[:8], right[8:]], axis=1)
    for v, ref in ((0, bias_ref), (2, top_ref)):
        pieces = []
        for b in range(SIDE):
            at = (b // 4) * SLICE
            for h in range(2):
                i = 4 * (b % 4) + v + h
                pieces.append(packed[i : i + 1, at : at + SLICE])
        ref[...] = jnp.concatenate(pieces, axis=1)


def slots_kernel(got_ref, at_ref, out_ref, data_scr):
    odd = lax.axis_index("col") % 2
    for second in range(SIDE):
        for first in range(SIDE):
            at = SUMS + first * SLICE
            block = got_ref[second, :, at : at + SLICE].astype(F32)
            r = jnp.where(odd == 1, first * SIDE + second, second * SIDE + first)
            data_scr[r] = jnp.concatenate([block[:CAP], block[CAP:]], axis=1)
    data = data_scr[...].reshape(ROWS * CAP, BLOCK).astype(BF16)
    out_ref[0] = dot(at_ref[...], data, NN).astype(BF16)


def tables_kernel(
    got_ref, meta_ref, medium_ref, out_far, medium_far, out_ref, wide_ref, out_sem, wide_sem
):
    for t in range(TABLES):
        wide_ref[t] = medium_ref[4 * t : 4 * t + 4].astype(F32).reshape(SLICE, NAMES)
    copies = begin((wide_ref, medium_far, wide_sem))
    row = subs((1024, SLOTS)).astype(F32)
    total = jnp.zeros((1024, BLOCK), F32)
    for c in range(COLS):
        meta = meta_ref[c, BATCH : BATCH + 16, :].astype(F32)
        name = jnp.concatenate(
            [meta[i : i + 1] * 32.0 + meta[2 + i : 3 + i] for i in range(2)], axis=1
        )
        total += dot(one_hot(name == row), got_ref[c], NN)
    out_ref[...] = total
    copies += begin((out_ref, out_far, out_sem))
    for copy in copies:
        copy.wait()


def sides():
    first, second = [], []
    for c in range(COLS):
        for k in range(SIDE):
            along_y = [(k * SIDE + y) * COLS + c for y in range(SIDE)]
            along_z = [(z * SIDE + k) * COLS + c for z in range(SIDE)]
            first.append(along_z if c % 2 else along_y)
            second.append(along_y if c % 2 else along_z)
    return first, second


def swap(value, axis, groups=None):
    return lax.all_to_all(
        value, axis, split_axis=0, concat_axis=0, tiled=True, axis_index_groups=groups
    )


def body(
    giant_table,
    look_row,
    look_owner,
    look_bag,
    look_count,
    medium_tables,
    medium_ids,
    medium_lengths,
    dense_features,
    click_labels,
    cross_left,
    cross_right,
    cross_bias,
    top_weight,
):
    first, second = sides()
    bias, weight = cross_bias.reshape(1, WIDE), top_weight.reshape(1, WIDE)
    live = jnp.arange(4)[None, None, :] < medium_lengths[:, :, None]
    ids = jnp.where(live, medium_ids, NAMES).reshape(BATCH, 4 * TABLES).astype(BF16)
    ids = jnp.pad(ids, ((0, 0), (0, BLOCK - 4 * TABLES)))
    own = jnp.concatenate([dense_features, ids], axis=1)
    names = jnp.concatenate([look_row // 32, look_row % 32]).astype(BF16).reshape(4, BLOCK)
    names = jnp.pad(names, ((0, 12), (0, 0)))

    look_row = look_row.reshape(1, SLOTS)
    send, at = call(
        route_kernel,
        (struct((ROWS, 2 * CAP, BLOCK), BF16), struct((SLOTS, ROWS * CAP), BF16)),
        look_count,
        look_row,
        look_owner.reshape(1, SLOTS),
        look_bag.reshape(1, SLOTS),
        giant_table,
        smem=(0,),
        vmem=60,
    )
    got = swap(send, "row")
    send = call(
        pool_kernel,
        struct((COLS, 48, BLOCK), BF16),
        got,
        own,
        names,
    )
    meta = swap(send, "col")
    send, x, counts, left_end, right_end, ends, own_meta = call(
        cross_kernel,
        (
            pltpu.VMEM((COLS, BATCH, 2 * RANK + BLOCK), BF16),
            pltpu.HBM((HOST, WIDE), BF16),
            pltpu.HBM((TABLES, HOST, NAMES), BF16),
            struct((BLOCK, RANK), BF16),
            struct((RANK, BLOCK), BF16),
            struct((2, BLOCK), F32),
            pltpu.VMEM((16, BLOCK), BF16),
        ),
        meta,
        jnp.swapaxes(medium_tables, 1, 2),
        cross_left,
        cross_right,
        weight,
        bias,
        far=(1, 2, 3, 4, 5),
        pinned=(1, 2, 3, 4, 5),
        far_outs=(1, 2),
        scratch=(
            pltpu.VMEM((TABLES, SLICE, NAMES), BF16),
            pltpu.VMEM((WIDE, RANK), BF16),
            pltpu.VMEM((RANK, WIDE), BF16),
            pltpu.VMEM((1, WIDE), F32),
            pltpu.VMEM((1, WIDE), F32),
            pltpu.VMEM((HOST, WIDE), BF16),
            pltpu.VMEM((TABLES, HOST, NAMES), BF16),
        ),
        copies=7,
        vmem=32,
    )
    got = swap(send, "col")
    send = call(
        residue_kernel,
        struct((COLS, BATCH, 2 * RANK + BLOCK), BF16),
        got,
        click_labels.reshape(1, BATCH),
    )
    ranks = swap(send, "col")
    send = call(
        part_kernel,
        struct((COLS, BATCH, BLOCK), BF16),
        ranks,
        left_end,
        right_end,
        ends,
        far_outs=(0,),
        scratch=(pltpu.VMEM((COLS, BATCH, BLOCK), BF16),),
        copies=1,
    )
    parts = swap(send, "col")
    send = call(
        grads_kernel,
        pltpu.VMEM((SIDE, SIDE, 16, SUMS + BLOCK), BF16),
        ranks,
        x,
        counts,
        cross_left,
        cross_right,
        weight,
        bias,
        far=range(1, 7),
        pinned=range(1, 7),
        scratch=(
            pltpu.VMEM((HOST, WIDE), BF16),
            pltpu.VMEM((TABLES, HOST, NAMES), BF16),
            pltpu.VMEM((WIDE, RANK), BF16),
            pltpu.VMEM((RANK, WIDE), BF16),
            pltpu.VMEM((1, WIDE), F32),
            pltpu.VMEM((1, WIDE), F32),
            pltpu.VMEM((RANK, WIDE), F32),
            pltpu.VMEM((HOST, WIDE), F32),
            pltpu.VMEM((2, WIDE), F32),
        ),
        copies=6,
        vmem=40,
        cost=pl.CostEstimate(flops=3 * 10**9, bytes_accessed=10**7, transcendentals=0),
    )
    send, sample_grads = call(
        back_kernel,
        (
            pltpu.VMEM((SIDE, SIDE, 16, SUMS + BLOCK), BF16),
            struct((BATCH, COLS * SLICE), BF16),
        ),
        parts,
        own_meta,
        send,
        free=(0, 2),
        far_outs=(1,),
        free_outs=(0,),
        scratch=(
            pltpu.VMEM((COLS, BATCH, BLOCK), BF16),
            pltpu.VMEM((SIDE, SIDE, 16, BLOCK), BF16),
            pltpu.VMEM((BATCH, COLS * SLICE), BF16),
        ),
        copies=4,
        alias={2: 0},
        vmem=40,
    )
    got = swap(send, ("row", "col"), first)
    send = call(middle_kernel, struct((SIDE, 16, SUMS + 512 + BLOCK), BF16), got)
    got = swap(send, ("row", "col"), second)
    left_grad, right_grad, bias_grad, top_grad, medium = call(
        last_kernel,
        (
            struct((16, RANK), F32),
            struct((8, WIDE), F32),
            struct((1, WIDE), F32),
            struct((1, WIDE), F32),
            struct((ROWS, 16, NAMES), BF16),
        ),
        got,
    )
    medium = swap(medium, "row")
    slots = call(
        slots_kernel,
        struct((1, SLOTS, BLOCK), BF16),
        got,
        at,
        scratch=(pltpu.VMEM((ROWS, CAP, BLOCK), F32),),
    )
    giant_grad, medium_grad = call(
        tables_kernel,
        (struct((1024, BLOCK), F32), struct((TABLES, SLICE, NAMES), F32)),
        lax.all_gather(slots, "col", axis=0, tiled=True),
        meta,
        medium,
        far_outs=(0, 1),
        scratch=(pltpu.VMEM((1024, BLOCK), F32), pltpu.VMEM((TABLES, SLICE, NAMES), F32)),
        copies=2,
    )
    medium_grad = jnp.swapaxes(medium_grad, 1, 2)
    return (
        sample_grads,
        giant_grad,
        medium_grad,
        left_grad,
        right_grad,
        bias_grad.reshape(WIDE),
        top_grad.reshape(WIDE),
    )


def solution(mesh):
    both = P(("row", "col"))
    placed = (
        P("row", None),
        both,
        P(("row", "col"), None),
        both,
        both,
        P(None, None, "col"),
        P(("row", "col"), None, None),
        P(("row", "col"), None),
        P(("row", "col"), None),
        both,
        P("col", None),
        P(None, "col"),
        P("col"),
        P("col"),
    )
    return jax.shard_map(
        body,
        mesh=mesh,
        in_specs=placed,
        out_specs=(
            P(("row", "col"), None),
            P("row", None),
            P(None, None, "col"),
            P(("col", "row"), None),
            P("row", "col"),
            P("col"),
            P("col"),
        ),
        check_vma=False,
    )
```
